512 devices in a mesh: patch: 64 (over z, y), grp: 8 (over x, core).
Axes of the slice: x: 4, y: 8, z: 8, core: 2. Of those that a mesh axis runs over, the one named last changes fastest.
Arguments:
- right_side: bfloat16 [16, 8192, 128], P('grp', 'patch'), may hold values from -6 to 6
- coefficient: bfloat16 [16, 8192, 128], P('grp', 'patch'), may hold values from 0.19921875 to 5
- row_counts: int32 [64], P('patch'), may hold values from 1 to 2, 80 in all
Outputs:
- solution: float32 [16, 8192, 128], P('grp', 'patch')
The draws below stay inside these ranges and needn't reach their ends.
Inputs may be any that keep to these rules, and one draw needn't show every extreme that they name: `row_counts`: each index of patch holds 1 to 2 rows, the same in every slab, 80 in all, and some index holds exactly 2.
All inputs are finite; a program needn't handle non-finite values. No bound on the sum of `row_counts` on one device may be relied on, other than what follows from the above.
Results may differ from the reference program's by a relative error of at most 0.0003.
Values sent between devices are 32-bit elements; how exact they have to be, the bound alone decides.
A program may use at most 64 MiB of HBM per device.

```python
import math
import jax
import jax.numpy as jnp
import numpy as np

PATCH = 64
CAP = 2
ZC = 128
CYCLES = 2
PRE = 2
POST = 1
COARSE_ITERS = 4
ROWS_TOTAL = 80
NX = 16
NYP = 8192
N_PATCH = 64


def shard_levels(rng, extent, split, smallest, top_value):
    def one(axis_at, shards_of):
        heights = jax.random.uniform(jax.random.fold_in(jax.random.fold_in(rng, 6), axis_at), (shards_of,), jnp.float32, smallest / len(split), top_value / len(split))
        return jnp.repeat(jnp.exp(heights), extent[axis_at] // shards_of).reshape((-1,) + (1,) * (len(extent) - axis_at - 1))

    gain = one(*split[0])
    for cut in split[1:]:
        gain = gain * one(*cut)
    return gain


def split_up(amount, total, reach, skew):
    portions = [(1 << 20) // math.isqrt(standing ** skew) + 1 for standing in range(2, amount + 1)]
    surplus, given = total - reach - (amount - 1), [1] * (amount - 1)
    while surplus > 0:
        candidates = [i for i in range(amount - 1) if given[i] < reach]
        whole, left = sum([portions[i] for i in candidates]), surplus
        for i in candidates:
            extra = min(reach - given[i], max(1, left * portions[i] // whole), surplus)
            given[i] = given[i] + extra
            surplus = surplus - extra
    return np.array([reach] + given)


def uneven_parts(rng, number_of, total, most, lean):
    if number_of == 2:
        one = jax.random.randint(rng, (), max(1, total - most), min(most, total - 1) + 1)
        return jnp.stack([one, total - one])
    tallies = jnp.asarray(split_up(number_of, total, most, lean), jnp.int32)
    pairs = (number_of - 1) // 2
    giver, taker = tallies[1:1 + 2 * pairs:2], tallies[2:2 + 2 * pairs:2]
    slack = jnp.minimum(giver - 1, most - taker)
    passed = jax.random.randint(jax.random.fold_in(rng, 1), (pairs,), 0, 1 << 20) % (slack + 1)
    tallies = tallies.at[1:1 + 2 * pairs:2].set(giver - passed).at[2:2 + 2 * pairs:2].set(taker + passed)
    return tallies[jax.random.permutation(jax.random.fold_in(rng, 2), number_of)]


def centred(rng, shape, scale, most, pieces=(), kind=jnp.bfloat16):
    gain = shard_levels(rng, shape, pieces, -0.22, 0.18) if pieces else 1.0
    drawn = jax.random.normal(rng, shape, jnp.float32) * scale * gain
    return jnp.minimum(jnp.maximum(drawn, -most), most).astype(kind)


def setup_inputs(seed: int = 0) -> dict:
    key_list = jax.random.split(jax.random.key(seed), 4)
    right_side = centred(key_list[0], (NX, NYP, ZC), 1.0, 6.0, ((0, 8), (1, 64)))
    coefficient = jnp.clip(jnp.exp(math.log(5.0) - 3.2227897 * jax.random.uniform(key_list[1], (NX, NYP, ZC), jnp.float32) ** shard_levels(key_list[1], (NX, NYP, ZC), ((0, 8), (1, 64)), -0.2, 0.2)), 0.19921875, 5.0).astype(jnp.bfloat16)
    row_counts = uneven_parts(key_list[2], N_PATCH, ROWS_TOTAL, CAP, 2).astype(jnp.int32)
    return {"right_side": right_side, "coefficient": coefficient, "row_counts": row_counts}


relax_factor = 0.8


def shifted(padded, axis_number, offset):
    spans = [slice(1, -1), slice(1, -1), slice(1, -1)]
    spans[axis_number] = slice(1 + offset, padded.shape[axis_number] - 1 + offset)
    return padded[tuple(spans)]


def apply_operator(padded_field, padded_coeff):
    center_field = shifted(padded_field, 0, 0)
    center_coeff = shifted(padded_coeff, 0, 0)
    result = jnp.zeros_like(center_field)
    for axis_number in range(3):
        for offset in (-1, 1):
            weight = 0.5 * (center_coeff + shifted(padded_coeff, axis_number, offset))
            result = result + weight * (center_field - shifted(padded_field, axis_number, offset))
    return result


def diagonal_of(padded_coeff):
    center_coeff = shifted(padded_coeff, 0, 0)
    result = jnp.zeros_like(center_coeff)
    for axis_number in range(3):
        for offset in (-1, 1):
            result = result + 0.5 * (center_coeff + shifted(padded_coeff, axis_number, offset))
    return result


def restrict(field):
    whole_x, whole_y, whole_z = field.shape
    blocks = field.reshape(whole_x // 2, 2, whole_y // 2, 2, whole_z // 2, 2)
    return 0.5 * jnp.sum(blocks, axis=(1, 3, 5))


def prolong(field):
    return jnp.repeat(jnp.repeat(jnp.repeat(field, 2, axis=0), 2, axis=1), 2, axis=2)


def compact_rows(row_counts):
    counts = row_counts.astype(jnp.int32)
    starts = (jnp.cumsum(counts) - counts).astype(jnp.int32)
    positions = jnp.arange(ROWS_TOTAL * PATCH, dtype=jnp.int32)
    patch_row = (positions // PATCH).astype(jnp.int32)
    owners = (jnp.sum((starts[None, :] <= patch_row[:, None]).astype(jnp.int32), axis=1) - 1).astype(jnp.int32)
    return ((owners * CAP + patch_row - starts[owners]) * PATCH + positions % PATCH).astype(jnp.int32)


def coarse_solve(coarse_rhs, coarse_padded):
    estimate = jnp.zeros_like(coarse_rhs)
    remain = coarse_rhs
    search = coarse_rhs
    norm_now = jnp.sum(remain * remain)
    for iteration in range(COARSE_ITERS):
        mapped = apply_operator(jnp.pad(search, 1), coarse_padded)
        step_size = norm_now / jnp.sum(search * mapped)
        estimate = estimate + step_size * search
        remain = remain - step_size * mapped
        norm_next = jnp.sum(remain * remain)
        search = remain + (norm_next / norm_now) * search
        norm_now = norm_next
    return estimate


def reference(right_side, coefficient, row_counts):
    row_index = compact_rows(row_counts)
    source = right_side[:, row_index, :].astype(jnp.float32)
    conduct = coefficient[:, row_index, :].astype(jnp.float32)
    padded_coeff = jnp.pad(conduct, 1)
    fine_diagonal = diagonal_of(padded_coeff)
    coarse_padded = jnp.pad(0.25 * restrict(conduct), 1)
    solution = jnp.zeros_like(source)
    for cycle_index in range(CYCLES):
        for sweep_index in range(PRE):
            mapped = apply_operator(jnp.pad(solution, 1), padded_coeff)
            solution = solution + relax_factor * (source - mapped) / fine_diagonal
        residual = source - apply_operator(jnp.pad(solution, 1), padded_coeff)
        correction = coarse_solve(restrict(residual), coarse_padded)
        solution = solution + prolong(correction)
        for sweep_index in range(POST):
            mapped = apply_operator(jnp.pad(solution, 1), padded_coeff)
            solution = solution + relax_factor * (source - mapped) / fine_diagonal
    return jnp.zeros(right_side.shape, jnp.float32).at[:, row_index, :].set(solution)
```

```python
import functools

import jax
import jax.numpy as jnp
from jax import lax
from jax.experimental import pallas as pl
from jax.experimental.pallas import tpu as pltpu
from jax.sharding import PartitionSpec as P

MESH = pl.DeviceIdType.MESH
CYCLES = 2
KRYLOV = 4
PATCH = 64
OWN = 128
HALO = 24
EXT = OWN + 2 * HALO
GUARD = 8
ROWS = EXT + 2 * GUARD
FIRST = GUARD + HALO
WIDE = 10
LANES = 128
TILES = EXT // 8
C_EXT = EXT // 2
C_ROWS = C_EXT + 2 * GUARD
C_TILES = C_EXT // 8
C_SENT = 48
C_SKIP = C_EXT - C_SENT
F32 = jnp.float32


def lane_roll(x, steps):
    return pltpu.roll(x, steps % LANES, axis=1)


def loop(count, body):
    def step(i, carry):
        body(i)
        return carry

    lax.fori_loop(0, count, step, 0)


def at_tile(i, offset):
    return pl.ds(offset + 8 * i, 8)


def kernel(n_patch, n_grp, rs_ref, cf_ref, count_ref, out_ref,
           own, last, low, high, kf, gain, diag, cx, cy, cz, u0, u1, total, coarse, packed, gathered,
           kc, ccx, ccy, ccz, cdiag, basis, part, parts,
           p_send, p_recv, b_send, b_recv, w_send, w_recv, c_send, c_recv, s_send, s_recv):
    half = n_grp // 2
    p = lax.axis_index("patch")
    g = lax.axis_index("grp")
    count = count_ref[0]
    two = count >= 2

    lane = lax.broadcasted_iota(jnp.int32, (8, LANES), 1)
    row = lax.broadcasted_iota(jnp.int32, (8, LANES), 0)
    even = lane % 2 == 0
    zero = jnp.zeros((8, LANES), F32)

    def inside(dp, dg):
        return (p + dp >= 0) & (p + dp < n_patch) & (g + dg >= 0) & (g + dg < n_grp)

    barrier = pltpu.get_barrier_semaphore()
    for dp in (-1, 1):
        for dg in (-2, -1, 1, 2):
            peer = (lax.rem(p + dp + n_patch, n_patch), lax.rem(g + dg + n_grp, n_grp))
            pl.semaphore_signal(barrier, inc=1, device_id=peer, device_id_type=MESH)
    for dg in range(1, n_grp):
        pl.semaphore_signal(barrier, inc=1, device_id=(p, lax.rem(g + dg, n_grp)), device_id_type=MESH)

    def greet(i):
        peer = (lax.rem(p + i + 1, n_patch), g)
        pl.semaphore_signal(barrier, inc=1, device_id=peer, device_id_type=MESH)

    loop(n_patch - 1, greet)

    for a, ref in ((0, cf_ref), (1, rs_ref)):
        for w in range(2):
            def stage(i, a=a, ref=ref, w=w):
                rows = pl.ds(16 * i, 16)
                at = lax.broadcasted_iota(jnp.int32, (16, LANES), 0) + 16 * i
                value = jnp.where(at < PATCH * count, ref[w, rows, :].astype(F32), 0.0)
                own[a, w, rows, :] = value
                kf[a, 4 + w, pl.ds(FIRST + 16 * i, 16), :] = value

            loop(OWN // 16, stage)
            last[a, w] = jnp.where(two, own[a, w, OWN - HALO:, :], own[a, w, PATCH - HALO:PATCH, :])

    guards = jnp.zeros((GUARD, LANES), F32)
    for ref in (u0, u1, cy):
        for w in range(WIDE):
            ref[w, 0:GUARD, :] = guards
            ref[w, ROWS - GUARD:, :] = guards
    for w in range(WIDE):
        kf[0, w, 0:GUARD, :] = guards
        kf[0, w, ROWS - GUARD:, :] = guards
    for j in range(half):
        for ref in (kc, ccy):
            ref[j, 0:GUARD, :] = guards
            ref[j, C_ROWS - GUARD:, :] = guards
        for m in range(KRYLOV):
            basis[m, j, 0:GUARD, :] = guards
            basis[m, j, C_ROWS - GUARD:, :] = guards

    def clear(ref):
        ref[...] = jnp.zeros(ref.shape, ref.dtype)

    @pl.when(p == 0)
    def _():
        clear(low)

    @pl.when(p == n_patch - 1)
    def _():
        clear(high)

    def outside(planes):
        for w in planes:
            def wipe(i, w=w):
                rows = at_tile(i, 0)
                kf[0, w, rows, :] = zero
                kf[1, w, rows, :] = zero
                u1[w, rows, :] = zero

            loop(ROWS // 8, wipe)
            for a in range(2):
                for ref in (low, high):
                    ref[a, w] = jnp.zeros((HALO, LANES), F32)

    @pl.when(g < 2)
    def _():
        outside((0, 1))

    @pl.when(g < 1)
    def _():
        outside((2, 3))

    @pl.when(g > n_grp - 3)
    def _():
        outside((8, 9))

    @pl.when(g > n_grp - 2)
    def _():
        outside((6, 7))

    pl.semaphore_wait(barrier, n_patch + n_grp + 6)

    def remote(src, dst, send, recv, peer):
        return pltpu.make_async_remote_copy(
            src_ref=src, dst_ref=dst, send_sem=send, recv_sem=recv, device_id=peer, device_id_type=MESH
        )

    first = []
    for dp, source, landing in ((0, own, kf), (1, last, low), (-1, own, high)):
        for dg in (-1, 1, -2, 2, 0):
            if dp == 0 and dg == 0:
                continue
            at = 4 - 2 * dg
            if abs(dg) == 2:
                w = 1 if dg == 2 else 0
                src, dst = source.at[0, w], landing.at[0, at + w]
                if dp == 0:
                    dst = landing.at[0, at + w, FIRST:FIRST + OWN, :]
                elif dp == -1:
                    src = source.at[0, w, 0:HALO, :]
            else:
                src, dst = source, landing.at[:, at:at + 2]
                if dp == 0:
                    dst = landing.at[:, at:at + 2, FIRST:FIRST + OWN, :]
                elif dp == -1:
                    src = source.at[:, :, 0:HALO, :]
            peer = (lax.rem(p + dp + n_patch, n_patch), lax.rem(g + dg + n_grp, n_grp))
            i = len(first)
            first.append((dp, dg, remote(src, dst, p_send.at[i], p_recv.at[i], peer)))

    def start(copies):
        for dp, dg, copy in copies:
            @pl.when(inside(dp, dg))
            def _(copy=copy):
                copy.start()

    def arrive(copies):
        for dp, dg, copy in copies:
            @pl.when(inside(-dp, -dg))
            def _(copy=copy):
                copy.wait_recv()

    def leave(copies):
        for dp, dg, copy in copies:
            @pl.when(inside(dp, dg))
            def _(copy=copy):
                copy.wait_send()

    start(first)
    arrive(first)

    def extend(a, w):
        kf[a, w, GUARD:FIRST, :] = low[a, w]
        upper = high[a, w]
        middle = slice(FIRST + PATCH, FIRST + PATCH + HALO)
        kf[a, w, middle, :] = jnp.where(two, kf[a, w, middle, :], upper)
        kf[a, w, FIRST + OWN:FIRST + OWN + HALO, :] = jnp.where(two, upper, 0.0)

    for w in range(1, 9):
        extend(0, w)
    for w in range(2, 8):
        extend(1, w)

    inner = slice(GUARD, GUARD + EXT)
    second = []
    for dg, src, dst in ((2, (0, 4), (0, 0)), (-2, (0, 5), (0, 9)), (2, (1, 5), (1, 1)), (-2, (1, 4), (1, 8))):
        i = len(second)
        peer = (p, lax.rem(g + dg + n_grp, n_grp))
        second.append((0, dg, remote(
            kf.at[src[0], src[1], inner, :], kf.at[dst[0], dst[1], inner, :], b_send.at[i], b_recv.at[i], peer)))

    def halve(slot, scale):
        def fold(i):
            s = total[pl.ds(GUARD + 16 * i, 8, stride=2), :] + total[pl.ds(GUARD + 16 * i + 1, 8, stride=2), :]
            coarse[at_tile(i, 0), :] = scale * (s + jnp.where(even, lane_roll(s, -1), lane_roll(s, 1)))

        loop(C_TILES, fold)

        def pack(i):
            value = jnp.where(even, coarse[at_tile(i, 0), :], coarse[at_tile(i, C_SKIP), :])
            packed[slot, at_tile(i, 0), :] = value
            gathered[slot, g, at_tile(i, 0), :] = value

        loop(C_SENT // 8, pack)
        return [
            remote(packed.at[slot], gathered.at[slot, g], c_send.at[slot, dg], c_recv.at[slot, dg],
                   (p, lax.rem(g + dg, n_grp)))
            for dg in range(1, n_grp)
        ]

    def unpack(slot, write):
        def upper(i):
            for j in range(half):
                a, b = gathered[slot, j, at_tile(i, 0), :], gathered[slot, j + half, at_tile(i, 0), :]
                write(j, at_tile(i, GUARD), jnp.where(even, a, lane_roll(b, 1)))

        def lower(i):
            for j in range(half):
                a, b = gathered[slot, j, at_tile(i, 8), :], gathered[slot, j + half, at_tile(i, 8), :]
                write(j, at_tile(i, GUARD + C_SENT), jnp.where(even, lane_roll(a, -1), b))

        loop(C_SENT // 8, upper)
        loop((C_EXT - C_SENT) // 8, lower)

    def sum_conduct(i):
        rows = at_tile(i, GUARD)
        total[rows, :] = kf[0, 4, rows, :] + kf[0, 5, rows, :]

    loop(TILES, sum_conduct)
    conduct_out = halve(0, 0.125)
    for copy in conduct_out:
        copy.start()

    def joined(a, b):
        return jnp.where((a > 0) & (b > 0), 0.5 * (a + b), 0.0)

    def set_diag(planes):
        def body(i):
            rows, before, after = at_tile(i, GUARD), at_tile(i, GUARD - 1), at_tile(i, GUARD + 1)
            for w in planes:
                k = kf[0, w, rows, :]
                near = kf[0, w - 1, rows, :] + kf[0, w + 1, rows, :] + kf[0, w, before, :] + kf[0, w, after, :]
                near = near + jnp.where(lane == LANES - 1, 0.0, lane_roll(k, -1))
                near = near + jnp.where(lane == 0, 0.0, lane_roll(k, 1))
                d = 3.0 * k + 0.5 * near
                diag[w, rows, :] = jnp.where(k > 0, d, 0.0)
                gain[w, rows, :] = jnp.where(k > 0, 0.8 / d, 0.0)

        loop(TILES, body)

    def set_weights(planes, between):
        def body(i):
            rows, after = at_tile(i, GUARD), at_tile(i, GUARD + 1)
            for w in between:
                cx[w, rows, :] = joined(kf[0, w, rows, :], kf[0, w + 1, rows, :])
            for w in planes:
                k = kf[0, w, rows, :]
                cy[w, rows, :] = joined(k, kf[0, w, after, :])
                cz[w, rows, :] = jnp.where(lane == LANES - 1, 0.0, joined(k, lane_roll(k, -1)))

        loop(TILES, body)

    def neighbours(u, i, planes):
        rows, before, after = at_tile(i, GUARD), at_tile(i, GUARD - 1), at_tile(i, GUARD + 1)
        centre = {w: u[w, rows, :] for w in range(planes[0] - 1, planes[-1] + 2)}
        result = {}
        for w in planes:
            z = cz[w, rows, :]
            s = cx[w, rows, :] * centre[w + 1] + cx[w - 1, rows, :] * centre[w - 1]
            s = s + cy[w, rows, :] * u[w, after, :] + cy[w, before, :] * u[w, before, :]
            s = s + z * lane_roll(centre[w], -1) + lane_roll(z * centre[w], 1)
            result[w] = s
        return rows, centre, result

    def sweep(src, dst, planes):
        def body(i):
            rows, centre, near = neighbours(src, i, planes)
            for w in planes:
                dst[w, rows, :] = 0.2 * centre[w] + gain[w, rows, :] * (kf[1, w, rows, :] + near[w])

        loop(TILES, body)

    def residual(src):
        def body(i):
            rows, centre, near = neighbours(src, i, (4, 5))
            r = [kf[1, w, rows, :] - diag[w, rows, :] * centre[w] + near[w] for w in (4, 5)]
            total[rows, :] = r[0] + r[1]

        loop(TILES, body)

    def set_coarse():
        def body(i):
            rows, before, after = at_tile(i, GUARD), at_tile(i, GUARD - 1), at_tile(i, GUARD + 1)
            k = [kc[j, rows, :] for j in range(half)]
            for j in range(half):
                beyond = k[j + 1] if j + 1 < half else jnp.where(even, lane_roll(k[0], -1), 0.0)
                ahead = k[j - 1] if j else jnp.where(even, 0.0, lane_roll(k[half - 1], 1))
                right = jnp.where(lane >= LANES - 2, 0.0, lane_roll(k[j], -2))
                left = jnp.where(lane < 2, 0.0, lane_roll(k[j], 2))
                up = kc[j, after, :]
                near = beyond + ahead + right + left + up + kc[j, before, :]
                cdiag[j, rows, :] = jnp.where(k[j] > 0, 3.0 * k[j] + 0.5 * near, 0.0)
                ccx[j, rows, :] = joined(k[j], beyond)
                ccy[j, rows, :] = joined(k[j], up)
                ccz[j, rows, :] = joined(k[j], right)

        loop(C_TILES, body)

    def krylov(cycle):
        sums = []
        for m in range(KRYLOV):
            def body(i, carry, m=m):
                rows, before, after = at_tile(i, GUARD), at_tile(i, GUARD - 1), at_tile(i, GUARD + 1)
                at = row + 8 * i
                mine = (at >= HALO // 2) & (at < HALO // 2 + PATCH // 2 * count)
                v = [basis[m, j, rows, :] for j in range(half)]
                square, cross = carry
                for j in range(half):
                    x, z = ccx[j, rows, :], ccz[j, rows, :]
                    s = x * v[j + 1] if j + 1 < half else x * lane_roll(v[0], -1)
                    if j:
                        s = s + ccx[j - 1, rows, :] * v[j - 1]
                    else:
                        s = s + lane_roll(ccx[half - 1, rows, :] * v[half - 1], 1)
                    s = s + ccy[j, rows, :] * basis[m, j, after, :] + ccy[j, before, :] * basis[m, j, before, :]
                    s = s + z * lane_roll(v[j], -2) + lane_roll(z * v[j], 2)
                    mapped = cdiag[j, rows, :] * v[j] - s
                    if m + 1 < KRYLOV:
                        basis[m + 1, j, rows, :] = mapped
                    masked = jnp.where(mine, v[j], 0.0)
                    square = square + masked * v[j]
                    cross = cross + masked * mapped
                return square, cross

            sums.extend(lax.fori_loop(0, C_TILES, body, (zero, zero)))
        line = jnp.zeros((1, LANES), F32)
        for m, value in enumerate(sums):
            line = jnp.where(lane[0:1] == m, jnp.sum(value), line)
        part[cycle] = line
        parts[cycle, p] = line

        def addressed(i):
            return remote(part.at[cycle], parts.at[cycle, p], s_send.at[cycle, i], s_recv.at[cycle, i],
                          (lax.rem(p + i + 1, n_patch), g))

        loop(n_patch - 1, lambda i: addressed(i).start())
        return addressed

    def coefficients(cycle, addressed):
        loop(n_patch - 1, lambda i: addressed(i).wait_recv())
        whole = jnp.sum(parts[cycle], axis=0)
        moment = [jnp.broadcast_to(whole[:, m:m + 1], (8, LANES)) for m in range(2 * KRYLOV)]
        matrix = [[moment[i + j + 1] for j in range(KRYLOV)] for i in range(KRYLOV)]
        right = moment[:KRYLOV]
        inverse = []
        for i in range(KRYLOV):
            pivot = matrix[i][i]
            inverse.append(jnp.where(pivot > 0, 1.0 / pivot, 0.0))
            for j in range(i + 1, KRYLOV):
                factor = matrix[i][j] * inverse[i]
                for l in range(j, KRYLOV):
                    matrix[j][l] = matrix[j][l] - factor * matrix[i][l]
                right[j] = right[j] - factor * right[i]
        answer = [None] * KRYLOV
        for i in reversed(range(KRYLOV)):
            value = right[i]
            for j in range(i + 1, KRYLOV):
                value = value - matrix[i][j] * answer[j]
            answer[i] = value * inverse[i]
        return answer

    def correct(u, answer, slabs):
        for s in slabs:
            at = g + s - 2
            valid = (at >= 0) & (at < n_grp)
            at = lax.rem(at + n_grp, n_grp)
            j, odd = lax.rem(at, half), at // half

            def body(i, s=s, valid=valid, j=j, odd=odd):
                value = zero
                for m in range(KRYLOV):
                    value = value + answer[m] * basis[m, j, at_tile(i, GUARD), :]
                moved = jnp.where(odd == 0, lane_roll(value, 1), lane_roll(value, -1))
                value = jnp.where(lane % 2 == odd, value, moved)
                value = jnp.where(valid, value, 0.0)
                for w in (2 * s, 2 * s + 1):
                    for a in range(2):
                        rows = pl.ds(GUARD + 16 * i + a, 8, stride=2)
                        u[w, rows, :] = u[w, rows, :] + value

            loop(C_TILES, body)

    def to_basis(j, rows, value):
        basis[0, j, rows, :] = value

    def to_conduct(j, rows, value):
        kc[j, rows, :] = value

    set_diag(range(2, 8))
    start(second)
    set_weights(range(3, 7), range(2, 7))

    def sweep_zero(i):
        rows = at_tile(i, GUARD)
        for w in range(2, 8):
            u0[w, rows, :] = gain[w, rows, :] * kf[1, w, rows, :]

    loop(TILES, sweep_zero)
    sweep(u0, u1, range(3, 7))
    residual(u1)
    first_out = halve(1, 0.5)
    for copy in first_out:
        copy.start()
    for copy in conduct_out:
        copy.wait_recv()
    unpack(0, to_conduct)
    set_coarse()
    for copy in first_out:
        copy.wait_recv()

    third = []
    for dg, src, dst in ((1, slice(4, 5), slice(2, 3)), (-1, slice(5, 6), slice(7, 8)),
                         (2, slice(4, 6), slice(0, 2)), (-2, slice(4, 6), slice(8, 10))):
        i = len(third)
        peer = (p, lax.rem(g + dg + n_grp, n_grp))
        third.append((0, dg, remote(u1.at[src, inner, :], u1.at[dst, inner, :], w_send.at[i], w_recv.at[i], peer)))
    start(third)
    unpack(1, to_basis)
    addressed = krylov(0)
    arrive(second)
    set_diag((1, 8))
    set_weights((1, 2, 7, 8), (0, 1, 7, 8))
    arrive(third)
    leave(third)
    answer = coefficients(0, addressed)
    correct(u1, answer, range(5))
    sweep(u1, u0, range(1, 9))

    sweep(u0, u1, range(2, 8))
    sweep(u1, u0, range(3, 7))
    residual(u0)
    second_out = halve(2, 0.5)
    for copy in second_out:
        copy.start()
    for copy in second_out:
        copy.wait_recv()
    unpack(2, to_basis)
    addressed_again = krylov(1)
    answer = coefficients(1, addressed_again)
    correct(u0, answer, range(1, 4))
    sweep(u0, u1, range(4, 6))

    def finish(i):
        for w in range(2):
            used = row + 8 * i < PATCH * count
            out_ref[w, at_tile(i, 0), :] = jnp.where(used, u1[4 + w, at_tile(i, FIRST), :], 0.0)

    loop(OWN // 8, finish)

    leave(first)
    leave(second)
    for copy in conduct_out + first_out + second_out:
        copy.wait_send()
    loop(n_patch - 1, lambda i: addressed(i).wait_send())
    loop(n_patch - 1, lambda i: addressed_again(i).wait_send())


def solution(mesh):
    n_patch, n_grp = mesh.shape["patch"], mesh.shape["grp"]
    half = n_grp // 2

    def per_device(right_side, coefficient, row_counts):
        fine = pltpu.VMEM((WIDE, ROWS, LANES), F32)
        level = pltpu.VMEM((half, C_ROWS, LANES), F32)
        dma = pltpu.SemaphoreType.DMA
        return pl.pallas_call(
            functools.partial(kernel, n_patch, n_grp),
            out_shape=jax.ShapeDtypeStruct(right_side.shape, F32),
            in_specs=[
                pl.BlockSpec(memory_space=pltpu.VMEM),
                pl.BlockSpec(memory_space=pltpu.VMEM),
                pl.BlockSpec(memory_space=pltpu.SMEM),
            ],
            out_specs=pl.BlockSpec(memory_space=pltpu.VMEM),
            scratch_shapes=[
                pltpu.VMEM((2, 2, OWN, LANES), F32),
                pltpu.VMEM((2, 2, HALO, LANES), F32),
                pltpu.VMEM((2, WIDE, HALO, LANES), F32),
                pltpu.VMEM((2, WIDE, HALO, LANES), F32),
                pltpu.VMEM((2, WIDE, ROWS, LANES), F32),
                fine, fine, fine, fine, fine, fine, fine,
                pltpu.VMEM((ROWS, LANES), F32),
                pltpu.VMEM((C_EXT, LANES), F32),
                pltpu.VMEM((3, C_SENT, LANES), F32),
                pltpu.VMEM((3, n_grp, C_SENT, LANES), F32),
                level, level, level, level, level,
                pltpu.VMEM((KRYLOV, half, C_ROWS, LANES), F32),
                pltpu.VMEM((CYCLES, 1, LANES), F32),
                pltpu.VMEM((CYCLES, n_patch, 1, LANES), F32),
                dma((14,)), dma((14,)), dma((4,)), dma((4,)), dma((4,)), dma((4,)),
                dma((3, n_grp)), dma((3, n_grp)),
                dma((CYCLES, n_patch - 1)), dma((CYCLES, n_patch - 1)),
            ],
            compiler_params=pltpu.CompilerParams(
                collective_id=0, has_side_effects=True, vmem_limit_bytes=40 << 20
            ),
        )(right_side, coefficient, row_counts)

    return jax.shard_map(
        per_device,
        mesh=mesh,
        in_specs=(P("grp", "patch", None), P("grp", "patch", None), P("patch")),
        out_specs=P("grp", "patch", None),
        check_vma=False,
    )
```

```python
import functools

import jax
import jax.numpy as jnp
from jax import lax
from jax.experimental import pallas as pl
from jax.experimental.pallas import tpu as pltpu
from jax.sharding import PartitionSpec as P

MESH = pl.DeviceIdType.MESH
CYCLES = 2
KRYLOV = 4
PATCH = 64
OWN = 128
HALO = 24
EXT = OWN + 2 * HALO
GUARD = 8
ROWS = EXT + 2 * GUARD
FIRST = GUARD + HALO
WIDE = 10
LANES = 128
TILES = EXT // 8
C_EXT = EXT // 2
C_ROWS = C_EXT + 2 * GUARD
C_TILES = C_EXT // 8
C_SENT = 48
C_SKIP = C_EXT - C_SENT
F32 = jnp.float32
GROUP = 22
C_GROUP = 11


def lane_roll(x, steps):
    return pltpu.roll(x, steps % LANES, axis=1)


def loop(count, body, group=1):
    if group >= count:
        for i in range(count):
            body(i)
        return

    def step(i, carry):
        for k in range(group):
            body(group * i + k)
        return carry

    lax.fori_loop(0, count // group, step, 0)


def at_tile(i, offset):
    return pl.ds(offset + 8 * i, 8)


def kernel(n_patch, n_grp, rs_ref, cf_ref, count_ref, out_ref,
           own, last, low, high, kf, gain, diag, cx, cy, cz, u0, u1, total, coarse, packed, gathered,
           kc, ccx, ccy, ccz, cdiag, basis, part, parts,
           p_send, p_recv, b_send, b_recv, w_send, w_recv, c_send, c_recv, s_send, s_recv):
    half = n_grp // 2
    p = lax.axis_index("patch")
    g = lax.axis_index("grp")
    count = count_ref[0]
    two = count >= 2

    lane = lax.broadcasted_iota(jnp.int32, (8, LANES), 1)
    row = lax.broadcasted_iota(jnp.int32, (8, LANES), 0)
    even = lane % 2 == 0
    zero = jnp.zeros((8, LANES), F32)

    def inside(dp, dg):
        return (p + dp >= 0) & (p + dp < n_patch) & (g + dg >= 0) & (g + dg < n_grp)

    barrier = pltpu.get_barrier_semaphore()
    for dp in (-1, 1):
        for dg in (-2, -1, 1, 2):
            peer = (lax.rem(p + dp + n_patch, n_patch), lax.rem(g + dg + n_grp, n_grp))
            pl.semaphore_signal(barrier, inc=1, device_id=peer, device_id_type=MESH)
    for dg in range(1, n_grp):
        pl.semaphore_signal(barrier, inc=1, device_id=(p, lax.rem(g + dg, n_grp)), device_id_type=MESH)

    def greet(i):
        peer = (lax.rem(p + i + 1, n_patch), g)
        pl.semaphore_signal(barrier, inc=1, device_id=peer, device_id_type=MESH)

    loop(n_patch - 1, greet)

    for a, ref in ((0, cf_ref), (1, rs_ref)):
        for w in range(2):
            def stage(i, a=a, ref=ref, w=w):
                rows = pl.ds(16 * i, 16)
                at = lax.broadcasted_iota(jnp.int32, (16, LANES), 0) + 16 * i
                value = jnp.where(at < PATCH * count, ref[w, rows, :].astype(F32), 0.0)
                own[a, w, rows, :] = value
                kf[a, 4 + w, pl.ds(FIRST + 16 * i, 16), :] = value

            loop(OWN // 16, stage)
            last[a, w] = jnp.where(two, own[a, w, OWN - HALO:, :], own[a, w, PATCH - HALO:PATCH, :])

    guards = jnp.zeros((GUARD, LANES), F32)
    for ref in (u0, u1, cy):
        for w in range(WIDE):
            ref[w, 0:GUARD, :] = guards
            ref[w, ROWS - GUARD:, :] = guards
    for w in range(WIDE):
        kf[0, w, 0:GUARD, :] = guards
        kf[0, w, ROWS - GUARD:, :] = guards
    for j in range(half):
        for ref in (kc, ccy):
            ref[j, 0:GUARD, :] = guards
            ref[j, C_ROWS - GUARD:, :] = guards
        for m in range(KRYLOV):
            basis[m, j, 0:GUARD, :] = guards
            basis[m, j, C_ROWS - GUARD:, :] = guards

    def clear(ref):
        ref[...] = jnp.zeros(ref.shape, ref.dtype)

    @pl.when(p == 0)
    def _():
        clear(low)

    @pl.when(p == n_patch - 1)
    def _():
        clear(high)

    def outside(planes):
        for w in planes:
            def wipe(i, w=w):
                rows = at_tile(i, 0)
                kf[0, w, rows, :] = zero
                kf[1, w, rows, :] = zero
                u1[w, rows, :] = zero

            loop(ROWS // 8, wipe)
            for a in range(2):
                for ref in (low, high):
                    ref[a, w] = jnp.zeros((HALO, LANES), F32)

    @pl.when(g < 2)
    def _():
        outside((0, 1))

    @pl.when(g < 1)
    def _():
        outside((2, 3))

    @pl.when(g > n_grp - 3)
    def _():
        outside((8, 9))

    @pl.when(g > n_grp - 2)
    def _():
        outside((6, 7))

    pl.semaphore_wait(barrier, n_patch + n_grp + 6)

    def remote(src, dst, send, recv, peer):
        return pltpu.make_async_remote_copy(
            src_ref=src, dst_ref=dst, send_sem=send, recv_sem=recv, device_id=peer, device_id_type=MESH
        )

    first = []
    for dp, source, landing in ((0, own, kf), (1, last, low), (-1, own, high)):
        for dg in (-1, 1, -2, 2, 0):
            if dp == 0 and dg == 0:
                continue
            at = 4 - 2 * dg
            if abs(dg) == 2:
                w = 1 if dg == 2 else 0
                src, dst = source.at[0, w], landing.at[0, at + w]
                if dp == 0:
                    dst = landing.at[0, at + w, FIRST:FIRST + OWN, :]
                elif dp == -1:
                    src = source.at[0, w, 0:HALO, :]
            else:
                src, dst = source, landing.at[:, at:at + 2]
                if dp == 0:
                    dst = landing.at[:, at:at + 2, FIRST:FIRST + OWN, :]
                elif dp == -1:
                    src = source.at[:, :, 0:HALO, :]
            peer = (lax.rem(p + dp + n_patch, n_patch), lax.rem(g + dg + n_grp, n_grp))
            i = len(first)
            first.append((dp, dg, remote(src, dst, p_send.at[i], p_recv.at[i], peer)))

    def start(copies):
        for dp, dg, copy in copies:
            @pl.when(inside(dp, dg))
            def _(copy=copy):
                copy.start()

    def arrive(copies):
        for dp, dg, copy in copies:
            @pl.when(inside(-dp, -dg))
            def _(copy=copy):
                copy.wait_recv()

    def leave(copies):
        for dp, dg, copy in copies:
            @pl.when(inside(dp, dg))
            def _(copy=copy):
                copy.wait_send()

    start(first)
    arrive(first)

    def extend(a, w):
        kf[a, w, GUARD:FIRST, :] = low[a, w]
        upper = high[a, w]
        middle = slice(FIRST + PATCH, FIRST + PATCH + HALO)
        kf[a, w, middle, :] = jnp.where(two, kf[a, w, middle, :], upper)
        kf[a, w, FIRST + OWN:FIRST + OWN + HALO, :] = jnp.where(two, upper, 0.0)

    for w in range(1, 9):
        extend(0, w)
    for w in range(2, 8):
        extend(1, w)

    inner = slice(GUARD, GUARD + EXT)
    second = []
    for dg, src, dst in ((2, (0, 4), (0, 0)), (-2, (0, 5), (0, 9)), (2, (1, 5), (1, 1)), (-2, (1, 4), (1, 8))):
        i = len(second)
        peer = (p, lax.rem(g + dg + n_grp, n_grp))
        second.append((0, dg, remote(
            kf.at[src[0], src[1], inner, :], kf.at[dst[0], dst[1], inner, :], b_send.at[i], b_recv.at[i], peer)))

    def halve(slot, scale):
        def fold(i):
            s = total[pl.ds(GUARD + 16 * i, 8, stride=2), :] + total[pl.ds(GUARD + 16 * i + 1, 8, stride=2), :]
            coarse[at_tile(i, 0), :] = scale * (s + jnp.where(even, lane_roll(s, -1), lane_roll(s, 1)))

        loop(C_TILES, fold, C_GROUP)

        def pack(i):
            value = jnp.where(even, coarse[at_tile(i, 0), :], coarse[at_tile(i, C_SKIP), :])
            packed[slot, at_tile(i, 0), :] = value
            gathered[slot, g, at_tile(i, 0), :] = value

        loop(C_SENT // 8, pack, C_GROUP)
        return [
            remote(packed.at[slot], gathered.at[slot, g], c_send.at[slot, dg], c_recv.at[slot, dg],
                   (p, lax.rem(g + dg, n_grp)))
            for dg in range(1, n_grp)
        ]

    def unpack(slot, write):
        def upper(i):
            for j in range(half):
                a, b = gathered[slot, j, at_tile(i, 0), :], gathered[slot, j + half, at_tile(i, 0), :]
                write(j, at_tile(i, GUARD), jnp.where(even, a, lane_roll(b, 1)))

        def lower(i):
            for j in range(half):
                a, b = gathered[slot, j, at_tile(i, 8), :], gathered[slot, j + half, at_tile(i, 8), :]
                write(j, at_tile(i, GUARD + C_SENT), jnp.where(even, lane_roll(a, -1), b))

        loop(C_SENT // 8, upper, C_GROUP)
        loop((C_EXT - C_SENT) // 8, lower, C_GROUP)

    def sum_conduct(i):
        rows = at_tile(i, GUARD)
        total[rows, :] = kf[0, 4, rows, :] + kf[0, 5, rows, :]

    loop(TILES, sum_conduct, GROUP)
    conduct_out = halve(0, 0.125)
    for copy in conduct_out:
        copy.start()

    def joined(a, b):
        return jnp.where((a > 0) & (b > 0), 0.5 * (a + b), 0.0)

    def set_diag(planes):
        def body(i):
            rows, before, after = at_tile(i, GUARD), at_tile(i, GUARD - 1), at_tile(i, GUARD + 1)
            for w in planes:
                k = kf[0, w, rows, :]
                near = kf[0, w - 1, rows, :] + kf[0, w + 1, rows, :] + kf[0, w, before, :] + kf[0, w, after, :]
                near = near + jnp.where(lane == LANES - 1, 0.0, lane_roll(k, -1))
                near = near + jnp.where(lane == 0, 0.0, lane_roll(k, 1))
                d = 3.0 * k + 0.5 * near
                diag[w, rows, :] = jnp.where(k > 0, d, 0.0)
                gain[w, rows, :] = jnp.where(k > 0, 0.8 / d, 0.0)

        loop(TILES, body, GROUP)

    def set_weights(planes, between):
        def body(i):
            rows, after = at_tile(i, GUARD), at_tile(i, GUARD + 1)
            for w in between:
                cx[w, rows, :] = joined(kf[0, w, rows, :], kf[0, w + 1, rows, :])
            for w in planes:
                k = kf[0, w, rows, :]
                cy[w, rows, :] = joined(k, kf[0, w, after, :])
                cz[w, rows, :] = jnp.where(lane == LANES - 1, 0.0, joined(k, lane_roll(k, -1)))

        loop(TILES, body, GROUP)

    def neighbours(u, i, planes):
        rows, before, after = at_tile(i, GUARD), at_tile(i, GUARD - 1), at_tile(i, GUARD + 1)
        centre = {w: u[w, rows, :] for w in range(planes[0] - 1, planes[-1] + 2)}
        result = {}
        for w in planes:
            z = cz[w, rows, :]
            s = cx[w, rows, :] * centre[w + 1] + cx[w - 1, rows, :] * centre[w - 1]
            s = s + cy[w, rows, :] * u[w, after, :] + cy[w, before, :] * u[w, before, :]
            s = s + z * lane_roll(centre[w], -1) + lane_roll(z * centre[w], 1)
            result[w] = s
        return rows, centre, result

    def sweep(src, dst, planes):
        def body(i):
            rows, centre, near = neighbours(src, i, planes)
            for w in planes:
                dst[w, rows, :] = 0.2 * centre[w] + gain[w, rows, :] * (kf[1, w, rows, :] + near[w])

        loop(TILES, body, GROUP)

    def residual(src):
        def body(i):
            rows, centre, near = neighbours(src, i, (4, 5))
            r = [kf[1, w, rows, :] - diag[w, rows, :] * centre[w] + near[w] for w in (4, 5)]
            total[rows, :] = r[0] + r[1]

        loop(TILES, body, GROUP)

    def set_coarse():
        def body(i):
            rows, before, after = at_tile(i, GUARD), at_tile(i, GUARD - 1), at_tile(i, GUARD + 1)
            k = [kc[j, rows, :] for j in range(half)]
            for j in range(half):
                beyond = k[j + 1] if j + 1 < half else jnp.where(even, lane_roll(k[0], -1), 0.0)
                ahead = k[j - 1] if j else jnp.where(even, 0.0, lane_roll(k[half - 1], 1))
                right = jnp.where(lane >= LANES - 2, 0.0, lane_roll(k[j], -2))
                left = jnp.where(lane < 2, 0.0, lane_roll(k[j], 2))
                up = kc[j, after, :]
                near = beyond + ahead + right + left + up + kc[j, before, :]
                cdiag[j, rows, :] = jnp.where(k[j] > 0, 3.0 * k[j] + 0.5 * near, 0.0)
                ccx[j, rows, :] = joined(k[j], beyond)
                ccy[j, rows, :] = joined(k[j], up)
                ccz[j, rows, :] = joined(k[j], right)

        loop(C_TILES, body, C_GROUP)

    def krylov(cycle):
        sums = []
        for m in range(KRYLOV):
            def body(i, carry, m=m):
                rows, before, after = at_tile(i, GUARD), at_tile(i, GUARD - 1), at_tile(i, GUARD + 1)
                at = row + 8 * i
                mine = (at >= HALO // 2) & (at < HALO // 2 + PATCH // 2 * count)
                v = [basis[m, j, rows, :] for j in range(half)]
                square, cross = carry
                for j in range(half):
                    x, z = ccx[j, rows, :], ccz[j, rows, :]
                    s = x * v[j + 1] if j + 1 < half else x * lane_roll(v[0], -1)
                    if j:
                        s = s + ccx[j - 1, rows, :] * v[j - 1]
                    else:
                        s = s + lane_roll(ccx[half - 1, rows, :] * v[half - 1], 1)
                    s = s + ccy[j, rows, :] * basis[m, j, after, :] + ccy[j, before, :] * basis[m, j, before, :]
                    s = s + z * lane_roll(v[j], -2) + lane_roll(z * v[j], 2)
                    mapped = cdiag[j, rows, :] * v[j] - s
                    if m + 1 < KRYLOV:
                        basis[m + 1, j, rows, :] = mapped
                    masked = jnp.where(mine, v[j], 0.0)
                    square = square + masked * v[j]
                    cross = cross + masked * mapped
                return square, cross

            if C_GROUP >= C_TILES:
                carry = (zero, zero)
                for i in range(C_TILES):
                    carry = body(i, carry)
                sums.extend(carry)
            else:
                sums.extend(lax.fori_loop(0, C_TILES, body, (zero, zero)))
        line = jnp.zeros((1, LANES), F32)
        for m, value in enumerate(sums):
            line = jnp.where(lane[0:1] == m, jnp.sum(value), line)
        part[cycle] = line
        parts[cycle, p] = line

        def addressed(i):
            return remote(part.at[cycle], parts.at[cycle, p], s_send.at[cycle, i], s_recv.at[cycle, i],
                          (lax.rem(p + i + 1, n_patch), g))

        loop(n_patch - 1, lambda i: addressed(i).start())
        return addressed

    def coefficients(cycle, addressed):
        loop(n_patch - 1, lambda i: addressed(i).wait_recv())
        whole = jnp.sum(parts[cycle], axis=0)
        moment = [jnp.broadcast_to(whole[:, m:m + 1], (8, LANES)) for m in range(2 * KRYLOV)]
        matrix = [[moment[i + j + 1] for j in range(KRYLOV)] for i in range(KRYLOV)]
        right = moment[:KRYLOV]
        inverse = []
        for i in range(KRYLOV):
            pivot = matrix[i][i]
            inverse.append(jnp.where(pivot > 0, 1.0 / pivot, 0.0))
            for j in range(i + 1, KRYLOV):
                factor = matrix[i][j] * inverse[i]
                for l in range(j, KRYLOV):
                    matrix[j][l] = matrix[j][l] - factor * matrix[i][l]
                right[j] = right[j] - factor * right[i]
        answer = [None] * KRYLOV
        for i in reversed(range(KRYLOV)):
            value = right[i]
            for j in range(i + 1, KRYLOV):
                value = value - matrix[i][j] * answer[j]
            answer[i] = value * inverse[i]
        return answer

    def correct(u, answer, slabs):
        for s in slabs:
            at = g + s - 2
            valid = (at >= 0) & (at < n_grp)
            at = lax.rem(at + n_grp, n_grp)
            j, odd = lax.rem(at, half), at // half

            def body(i, s=s, valid=valid, j=j, odd=odd):
                value = zero
                for m in range(KRYLOV):
                    value = value + answer[m] * basis[m, j, at_tile(i, GUARD), :]
                moved = jnp.where(odd == 0, lane_roll(value, 1), lane_roll(value, -1))
                value = jnp.where(lane % 2 == odd, value, moved)
                value = jnp.where(valid, value, 0.0)
                for w in (2 * s, 2 * s + 1):
                    for a in range(2):
                        rows = pl.ds(GUARD + 16 * i + a, 8, stride=2)
                        u[w, rows, :] = u[w, rows, :] + value

            loop(C_TILES, body, C_GROUP)

    def to_basis(j, rows, value):
        basis[0, j, rows, :] = value

    def to_conduct(j, rows, value):
        kc[j, rows, :] = value

    set_diag(range(2, 8))
    start(second)
    set_weights(range(3, 7), range(2, 7))

    def sweep_zero(i):
        rows = at_tile(i, GUARD)
        for w in range(2, 8):
            u0[w, rows, :] = gain[w, rows, :] * kf[1, w, rows, :]

    loop(TILES, sweep_zero, GROUP)
    sweep(u0, u1, range(3, 7))
    residual(u1)
    first_out = halve(1, 0.5)
    for copy in first_out:
        copy.start()
    for copy in conduct_out:
        copy.wait_recv()
    unpack(0, to_conduct)
    set_coarse()
    for copy in first_out:
        copy.wait_recv()

    third = []
    for dg, src, dst in ((1, slice(4, 5), slice(2, 3)), (-1, slice(5, 6), slice(7, 8)),
                         (2, slice(4, 6), slice(0, 2)), (-2, slice(4, 6), slice(8, 10))):
        i = len(third)
        peer = (p, lax.rem(g + dg + n_grp, n_grp))
        third.append((0, dg, remote(u1.at[src, inner, :], u1.at[dst, inner, :], w_send.at[i], w_recv.at[i], peer)))
    start(third)
    unpack(1, to_basis)
    addressed = krylov(0)
    arrive(second)
    set_diag((1, 8))
    set_weights((1, 2, 7, 8), (0, 1, 7, 8))
    arrive(third)
    leave(third)
    answer = coefficients(0, addressed)
    correct(u1, answer, range(5))
    sweep(u1, u0, range(1, 9))

    sweep(u0, u1, range(2, 8))
    sweep(u1, u0, range(3, 7))
    residual(u0)
    second_out = halve(2, 0.5)
    for copy in second_out:
        copy.start()
    for copy in second_out:
        copy.wait_recv()
    unpack(2, to_basis)
    addressed_again = krylov(1)
    answer = coefficients(1, addressed_again)
    correct(u0, answer, range(1, 4))
    sweep(u0, u1, range(4, 6))

    def finish(i):
        for w in range(2):
            used = row + 8 * i < PATCH * count
            out_ref[w, at_tile(i, 0), :] = jnp.where(used, u1[4 + w, at_tile(i, FIRST), :], 0.0)

    loop(OWN // 8, finish)

    leave(first)
    leave(second)
    for copy in conduct_out + first_out + second_out:
        copy.wait_send()
    loop(n_patch - 1, lambda i: addressed(i).wait_send())
    loop(n_patch - 1, lambda i: addressed_again(i).wait_send())


def solution(mesh):
    n_patch, n_grp = mesh.shape["patch"], mesh.shape["grp"]
    half = n_grp // 2

    def per_device(right_side, coefficient, row_counts):
        fine = pltpu.VMEM((WIDE, ROWS, LANES), F32)
        level = pltpu.VMEM((half, C_ROWS, LANES), F32)
        dma = pltpu.SemaphoreType.DMA
        return pl.pallas_call(
            functools.partial(kernel, n_patch, n_grp),
            out_shape=jax.ShapeDtypeStruct(right_side.shape, F32),
            in_specs=[
                pl.BlockSpec(memory_space=pltpu.VMEM),
                pl.BlockSpec(memory_space=pltpu.VMEM),
                pl.BlockSpec(memory_space=pltpu.SMEM),
            ],
            out_specs=pl.BlockSpec(memory_space=pltpu.VMEM),
            scratch_shapes=[
                pltpu.VMEM((2, 2, OWN, LANES), F32),
                pltpu.VMEM((2, 2, HALO, LANES), F32),
                pltpu.VMEM((2, WIDE, HALO, LANES), F32),
                pltpu.VMEM((2, WIDE, HALO, LANES), F32),
                pltpu.VMEM((2, WIDE, ROWS, LANES), F32),
                fine, fine, fine, fine, fine, fine, fine,
                pltpu.VMEM((ROWS, LANES), F32),
                pltpu.VMEM((C_EXT, LANES), F32),
                pltpu.VMEM((3, C_SENT, LANES), F32),
                pltpu.VMEM((3, n_grp, C_SENT, LANES), F32),
                level, level, level, level, level,
                pltpu.VMEM((KRYLOV, half, C_ROWS, LANES), F32),
                pltpu.VMEM((CYCLES, 1, LANES), F32),
                pltpu.VMEM((CYCLES, n_patch, 1, LANES), F32),
                dma((14,)), dma((14,)), dma((4,)), dma((4,)), dma((4,)), dma((4,)),
                dma((3, n_grp)), dma((3, n_grp)),
                dma((CYCLES, n_patch - 1)), dma((CYCLES, n_patch - 1)),
            ],
            compiler_params=pltpu.CompilerParams(
                collective_id=0, has_side_effects=True, vmem_limit_bytes=40 << 20
            ),
        )(right_side, coefficient, row_counts)

    return jax.shard_map(
        per_device,
        mesh=mesh,
        in_specs=(P("grp", "patch", None), P("grp", "patch", None), P("patch")),
        out_specs=P("grp", "patch", None),
        check_vma=False,
    )
```

```python
import functools

import jax
import jax.numpy as jnp
from jax import lax
from jax.experimental import pallas as pl
from jax.experimental.pallas import tpu as pltpu
from jax.sharding import PartitionSpec as P

MESH = pl.DeviceIdType.MESH
CYCLES = 2
KRYLOV = 4
PATCH = 64
CAP = 2
OWN = 128
HALO = 24
EXT = OWN + 2 * HALO
GUARD = 8
ROWS = EXT + 2 * GUARD
FIRST = GUARD + HALO
WIDE = 10
LANES = 128
ALL = range(EXT // 8)
MOST = range(1, EXT // 8 - 1)
MINE = range(HALO // 8, (HALO + OWN) // 8)
C_EXT = EXT // 2
C_ROWS = C_EXT + 2 * GUARD
C_ALL = range(C_EXT // 8)
C_MOST = range(1, C_EXT // 8 - 1)
C_SENT = 48
F32 = jnp.float32
SIDE = 8


def lane_roll(x, steps):
    return pltpu.roll(x, steps % LANES, axis=1)


def loop(count, body):
    def step(i, carry):
        body(i)
        return carry

    lax.fori_loop(0, count, step, 0)


def each(tiles, body):
    for i in tiles:
        body(i)


def farthest_first(i):
    return SIDE // 2 + jnp.where(i % 2 == 0, i // 2, -((i + 1) // 2))


def at_tile(i, offset):
    return pl.ds(offset + 8 * i, 8)


def kernel(n_patch, n_grp, rs_hbm, cf_hbm, count_hbm, out_ref,
           rs_ref, cf_ref, count_ref, in_sem, own, last, low, high, kf, gain, diag, cx, cy, cz, u0, u1, total, coarse, packed, gathered,
           kc, ccx, ccy, ccz, cdiag, basis, part, parts,
           p_send, p_recv, b_send, b_recv, w_send, w_recv, c_send, c_recv, s_send, s_recv):
    half = n_grp // 2
    p = lax.axis_index("patch")
    g = lax.axis_index("grp")
    loads = [
        pltpu.make_async_copy(src, dst, in_sem.at[i])
        for i, (src, dst) in enumerate(((count_hbm, count_ref), (cf_hbm, cf_ref), (rs_hbm, rs_ref)))
    ]
    for copy in loads:
        copy.start()

    lane = lax.broadcasted_iota(jnp.int32, (8, LANES), 1)
    row = lax.broadcasted_iota(jnp.int32, (8, LANES), 0)
    even = lane % 2 == 0
    zero = jnp.zeros((8, LANES), F32)

    def inside(dp, dg):
        return (p + dp >= 0) & (p + dp < n_patch) & (g + dg >= 0) & (g + dg < n_grp)

    barrier = pltpu.get_barrier_semaphore()
    for dp in (-1, 1):
        for dg in (-2, -1, 1, 2):
            peer = (lax.rem(p + dp + n_patch, n_patch), lax.rem(g + dg + n_grp, n_grp))
            pl.semaphore_signal(barrier, inc=1, device_id=peer, device_id_type=MESH)
    for dg in range(1, n_grp):
        pl.semaphore_signal(barrier, inc=1, device_id=(p, lax.rem(g + dg, n_grp)), device_id_type=MESH)

    def greet(i):
        peer = (lax.rem(p + i + 1, n_patch), g)
        pl.semaphore_signal(barrier, inc=1, device_id=peer, device_id_type=MESH)

    loop(n_patch - 1, greet)
    for copy in loads:
        copy.wait()
    count = count_ref[0]
    two = count >= 2

    for a, ref in ((0, cf_ref), (1, rs_ref)):
        for w in range(2):
            for half_rows in range(CAP):
                rows = slice(PATCH * half_rows, PATCH * (half_rows + 1))
                value = ref[w, rows, :].astype(F32)
                if half_rows:
                    value = jnp.where(two, value, 0.0)
                own[a, w, rows, :] = value
                kf[a, 4 + w, FIRST + PATCH * half_rows:FIRST + PATCH * (half_rows + 1), :] = value
            last[a, w] = jnp.where(two, own[a, w, OWN - HALO:, :], own[a, w, PATCH - HALO:PATCH, :])

    guards = jnp.zeros((GUARD, LANES), F32)
    for ref in (u0, u1, cy):
        for w in range(WIDE):
            ref[w, 0:GUARD, :] = guards
            ref[w, ROWS - GUARD:, :] = guards
    for w in range(WIDE):
        kf[0, w, 0:GUARD, :] = guards
        kf[0, w, ROWS - GUARD:, :] = guards
    for j in range(half):
        for ref in (kc, ccy):
            ref[j, 0:GUARD, :] = guards
            ref[j, C_ROWS - GUARD:, :] = guards
        for m in range(KRYLOV):
            basis[m, j, 0:GUARD, :] = guards
            basis[m, j, C_ROWS - GUARD:, :] = guards

    def clear(ref):
        ref[...] = jnp.zeros(ref.shape, ref.dtype)

    @pl.when(p == 0)
    def _():
        clear(low)

    @pl.when(p == n_patch - 1)
    def _():
        clear(high)

    def outside(planes):
        for w in planes:
            def wipe(i, w=w):
                rows = at_tile(i, 0)
                kf[0, w, rows, :] = zero
                kf[1, w, rows, :] = zero
                u1[w, rows, :] = zero

            loop(ROWS // 8, wipe)
            for a in range(2):
                for ref in (low, high):
                    ref[a, w] = jnp.zeros((HALO, LANES), F32)

    @pl.when(g < 2)
    def _():
        outside((0, 1))

    @pl.when(g < 1)
    def _():
        outside((2, 3))

    @pl.when(g > n_grp - 3)
    def _():
        outside((8, 9))

    @pl.when(g > n_grp - 2)
    def _():
        outside((6, 7))

    pl.semaphore_wait(barrier, n_patch + n_grp + 6)

    def remote(src, dst, send, recv, peer):
        return pltpu.make_async_remote_copy(
            src_ref=src, dst_ref=dst, send_sem=send, recv_sem=recv, device_id=peer, device_id_type=MESH
        )

    first = []
    for a in range(2):
        for dp, source, landing in ((0, own, kf), (1, last, low), (-1, own, high)):
            for dg in (-2, 2, -1, 1, 0):
                if (dp == 0 and dg == 0) or (a == 1 and abs(dg) == 2):
                    continue
                at = 4 - 2 * dg
                w = {2: slice(1, 2), -2: slice(0, 1)}.get(dg, slice(0, 2))
                src, dst = source.at[a, w], landing.at[a, at + w.start:at + w.stop]
                if dp == 0:
                    dst = landing.at[a, at + w.start:at + w.stop, FIRST:FIRST + OWN, :]
                elif dp == -1:
                    src = source.at[a, w, 0:HALO, :]
                peer = (lax.rem(p + dp + n_patch, n_patch), lax.rem(g + dg + n_grp, n_grp))
                i = len(first)
                first.append((dp, dg, remote(src, dst, p_send.at[i], p_recv.at[i], peer)))
    conduct_halo, source_halo = first[:14], first[14:]

    def start(copies):
        for dp, dg, copy in copies:
            @pl.when(inside(dp, dg))
            def _(copy=copy):
                copy.start()

    def arrive(copies):
        for dp, dg, copy in copies:
            @pl.when(inside(-dp, -dg))
            def _(copy=copy):
                copy.wait_recv()

    def leave(copies):
        for dp, dg, copy in copies:
            @pl.when(inside(dp, dg))
            def _(copy=copy):
                copy.wait_send()

    start(conduct_halo)
    start(source_halo)
    arrive(conduct_halo)

    def extend(a, w):
        kf[a, w, GUARD:FIRST, :] = low[a, w]
        upper = high[a, w]
        middle = slice(FIRST + PATCH, FIRST + PATCH + HALO)
        kf[a, w, middle, :] = jnp.where(two, kf[a, w, middle, :], upper)
        kf[a, w, FIRST + OWN:FIRST + OWN + HALO, :] = jnp.where(two, upper, 0.0)

    for w in range(1, 9):
        extend(0, w)

    inner = slice(GUARD + 8, GUARD + EXT - 8)
    second = []
    for dg, src, dst in ((2, (0, 4), (0, 0)), (-2, (0, 5), (0, 9)), (2, (1, 5), (1, 1)), (-2, (1, 4), (1, 8))):
        i = len(second)
        peer = (p, lax.rem(g + dg + n_grp, n_grp))
        second.append((0, dg, remote(
            kf.at[src[0], src[1], inner, :], kf.at[dst[0], dst[1], inner, :], b_send.at[i], b_recv.at[i], peer)))

    def halve(slot, scale, tiles):
        top, sent, skip = window(tiles)

        def fold(i):
            s = total[pl.ds(GUARD + 16 * i, 8, stride=2), :] + total[pl.ds(GUARD + 16 * i + 1, 8, stride=2), :]
            coarse[at_tile(i, 0), :] = scale * (s + jnp.where(even, lane_roll(s, -1), lane_roll(s, 1)))

        each(tiles, fold)

        def pack(i):
            value = jnp.where(even, coarse[at_tile(i, top), :], coarse[at_tile(i, top + skip), :])
            packed[slot, at_tile(i, 0), :] = value
            gathered[slot, g, at_tile(i, 0), :] = value

        each(range(sent // 8), pack)
        return [
            remote(packed.at[slot, 0:sent, :], gathered.at[slot, g, 0:sent, :], c_send.at[slot, dg],
                   c_recv.at[slot, dg], (p, lax.rem(g + dg, n_grp)))
            for dg in sorted(range(1, n_grp), key=lambda d: (-min(d, n_grp - d), d))
        ]

    def window(tiles):
        rows = 8 * len(tiles)
        sent = (rows // 2 + 7) // 8 * 8
        return 8 * tiles[0], sent, rows - sent

    def unpack(slot, write, tiles):
        top, sent, skip = window(tiles)

        def upper(i):
            for j in range(half):
                a, b = gathered[slot, j, at_tile(i, 0), :], gathered[slot, j + half, at_tile(i, 0), :]
                write(j, at_tile(i, GUARD + top), jnp.where(even, a, lane_roll(b, 1)))

        def lower(i):
            for j in range(half):
                rows = at_tile(i, sent - skip)
                a, b = gathered[slot, j, rows, :], gathered[slot, j + half, rows, :]
                write(j, at_tile(i, GUARD + top + sent), jnp.where(even, lane_roll(a, -1), b))

        each(range(sent // 8), upper)
        each(range(skip // 8), lower)

    def sum_conduct(i):
        rows = at_tile(i, GUARD)
        total[rows, :] = kf[0, 4, rows, :] + kf[0, 5, rows, :]

    each(ALL, sum_conduct)
    conduct_out = halve(0, 0.125, C_ALL)
    for copy in conduct_out:
        copy.start()

    def joined(a, b):
        return jnp.where((a > 0) & (b > 0), 0.5 * (a + b), 0.0)

    def set_diag(planes, tiles):
        def body(i):
            rows, before, after = at_tile(i, GUARD), at_tile(i, GUARD - 1), at_tile(i, GUARD + 1)
            for w in planes:
                k = kf[0, w, rows, :]
                near = kf[0, w - 1, rows, :] + kf[0, w + 1, rows, :] + kf[0, w, before, :] + kf[0, w, after, :]
                near = near + jnp.where(lane == LANES - 1, 0.0, lane_roll(k, -1))
                near = near + jnp.where(lane == 0, 0.0, lane_roll(k, 1))
                d = 3.0 * k + 0.5 * near
                diag[w, rows, :] = jnp.where(k > 0, d, 0.0)
                gain[w, rows, :] = jnp.where(k > 0, 0.8 / d, 0.0)

        each(tiles, body)

    def set_weights(planes, between, tiles):
        def body(i):
            rows, after = at_tile(i, GUARD), at_tile(i, GUARD + 1)
            for w in between:
                cx[w, rows, :] = joined(kf[0, w, rows, :], kf[0, w + 1, rows, :])
            for w in planes:
                k = kf[0, w, rows, :]
                cy[w, rows, :] = joined(k, kf[0, w, after, :])
                cz[w, rows, :] = jnp.where(lane == LANES - 1, 0.0, joined(k, lane_roll(k, -1)))

        each(tiles, body)

    def neighbours(u, i, planes):
        rows, before, after = at_tile(i, GUARD), at_tile(i, GUARD - 1), at_tile(i, GUARD + 1)
        centre = {w: u[w, rows, :] for w in range(planes[0] - 1, planes[-1] + 2)}
        result = {}
        for w in planes:
            z = cz[w, rows, :]
            s = cx[w, rows, :] * centre[w + 1] + cx[w - 1, rows, :] * centre[w - 1]
            s = s + cy[w, rows, :] * u[w, after, :] + cy[w, before, :] * u[w, before, :]
            s = s + z * lane_roll(centre[w], -1) + lane_roll(z * centre[w], 1)
            result[w] = s
        return rows, centre, result

    def sweep(src, dst, planes, tiles):
        def body(i):
            rows, centre, near = neighbours(src, i, planes)
            for w in planes:
                dst[w, rows, :] = 0.2 * centre[w] + gain[w, rows, :] * (kf[1, w, rows, :] + near[w])

        each(tiles, body)

    def residual(src, tiles):
        def body(i):
            rows, centre, near = neighbours(src, i, (4, 5))
            r = [kf[1, w, rows, :] - diag[w, rows, :] * centre[w] + near[w] for w in (4, 5)]
            total[rows, :] = r[0] + r[1]

        each(tiles, body)

    def set_coarse():
        def body(i):
            rows, before, after = at_tile(i, GUARD), at_tile(i, GUARD - 1), at_tile(i, GUARD + 1)
            k = [kc[j, rows, :] for j in range(half)]
            for j in range(half):
                beyond = k[j + 1] if j + 1 < half else jnp.where(even, lane_roll(k[0], -1), 0.0)
                ahead = k[j - 1] if j else jnp.where(even, 0.0, lane_roll(k[half - 1], 1))
                right = jnp.where(lane >= LANES - 2, 0.0, lane_roll(k[j], -2))
                left = jnp.where(lane < 2, 0.0, lane_roll(k[j], 2))
                up = kc[j, after, :]
                near = beyond + ahead + right + left + up + kc[j, before, :]
                cdiag[j, rows, :] = jnp.where(k[j] > 0, 3.0 * k[j] + 0.5 * near, 0.0)
                ccx[j, rows, :] = joined(k[j], beyond)
                ccy[j, rows, :] = joined(k[j], up)
                ccz[j, rows, :] = joined(k[j], right)

        each(C_ALL, body)

    def krylov(cycle, tiles):
        sums = []
        for m in range(KRYLOV):
            def body(i, carry, m=m):
                rows, before, after = at_tile(i, GUARD), at_tile(i, GUARD - 1), at_tile(i, GUARD + 1)
                at = row + 8 * i
                mine = (at >= HALO // 2) & (at < HALO // 2 + PATCH // 2 * count)
                v = [basis[m, j, rows, :] for j in range(half)]
                square, cross = carry
                for j in range(half):
                    x, z = ccx[j, rows, :], ccz[j, rows, :]
                    s = x * v[j + 1] if j + 1 < half else x * lane_roll(v[0], -1)
                    if j:
                        s = s + ccx[j - 1, rows, :] * v[j - 1]
                    else:
                        s = s + lane_roll(ccx[half - 1, rows, :] * v[half - 1], 1)
                    s = s + ccy[j, rows, :] * basis[m, j, after, :] + ccy[j, before, :] * basis[m, j, before, :]
                    s = s + z * lane_roll(v[j], -2) + lane_roll(z * v[j], 2)
                    mapped = cdiag[j, rows, :] * v[j] - s
                    if m + 1 < KRYLOV:
                        basis[m + 1, j, rows, :] = mapped
                    masked = jnp.where(mine, v[j], 0.0)
                    square = square + masked * v[j]
                    cross = cross + masked * mapped
                return square, cross

            carry = (zero, zero)
            for i in tiles:
                carry = body(i, carry)
            sums.extend(carry)
        stacked = jnp.concatenate([jnp.sum(value, axis=0, keepdims=True) for value in sums], axis=0)
        stacked = jnp.where(lane == row, jnp.sum(stacked, axis=1, keepdims=True), 0.0)
        line = jnp.sum(stacked, axis=0, keepdims=True)
        part[cycle] = line
        parts[cycle, p] = line

        def send(i):
            dz, dy = farthest_first(i // SIDE), farthest_first(i % SIDE)
            peer = (lax.rem(p // SIDE + dz, n_patch // SIDE) * SIDE + lax.rem(p % SIDE + dy, SIDE), g)
            remote(part.at[cycle], parts.at[cycle, p], s_send.at[cycle], s_recv.at[cycle], peer).start()

        loop(n_patch - 1, send)

    def everyone(cycle):
        rows = parts.at[cycle, 0:n_patch - 1]
        return remote(rows, rows, s_send.at[cycle], s_recv.at[cycle], (lax.rem(p + 1, n_patch), g))

    def coefficients(cycle):
        everyone(cycle).wait_recv()
        whole = jnp.sum(parts[cycle], axis=0)
        moment = [jnp.broadcast_to(whole[:, m:m + 1], (8, LANES)) for m in range(2 * KRYLOV)]
        matrix = [[moment[i + j + 1] for j in range(KRYLOV)] for i in range(KRYLOV)]
        right = moment[:KRYLOV]
        inverse = []
        for i in range(KRYLOV):
            pivot = matrix[i][i]
            inverse.append(jnp.where(pivot > 0, 1.0 / pivot, 0.0))
            for j in range(i + 1, KRYLOV):
                factor = matrix[i][j] * inverse[i]
                for l in range(j, KRYLOV):
                    matrix[j][l] = matrix[j][l] - factor * matrix[i][l]
                right[j] = right[j] - factor * right[i]
        answer = [None] * KRYLOV
        for i in reversed(range(KRYLOV)):
            value = right[i]
            for j in range(i + 1, KRYLOV):
                value = value - matrix[i][j] * answer[j]
            answer[i] = value * inverse[i]
        return answer

    def correct(u, answer, slabs, tiles):
        for s in slabs:
            at = g + s - 2
            valid = (at >= 0) & (at < n_grp)
            at = lax.rem(at + n_grp, n_grp)
            j, odd = lax.rem(at, half), at // half

            def body(i, s=s, valid=valid, j=j, odd=odd):
                value = zero
                for m in range(KRYLOV):
                    value = value + answer[m] * basis[m, j, at_tile(i, GUARD), :]
                moved = jnp.where(odd == 0, lane_roll(value, 1), lane_roll(value, -1))
                value = jnp.where(lane % 2 == odd, value, moved)
                value = jnp.where(valid, value, 0.0)
                for w in (2 * s, 2 * s + 1):
                    for a in range(2):
                        rows = pl.ds(GUARD + 16 * i + a, 8, stride=2)
                        u[w, rows, :] = u[w, rows, :] + value

            each(tiles, body)

    def to_basis(j, rows, value):
        basis[0, j, rows, :] = value

    def to_conduct(j, rows, value):
        kc[j, rows, :] = value

    set_diag(range(2, 8), ALL)
    set_weights(range(3, 7), range(2, 7), ALL)
    arrive(source_halo)
    for w in range(2, 8):
        extend(1, w)

    def sweep_zero(i):
        rows = at_tile(i, GUARD)
        for w in range(2, 8):
            u0[w, rows, :] = gain[w, rows, :] * kf[1, w, rows, :]

    each(ALL, sweep_zero)
    sweep(u0, u1, range(3, 7), ALL)
    residual(u1, ALL)
    first_out = halve(1, 0.5, C_ALL)
    for copy in first_out:
        copy.start()
    for copy in conduct_out:
        copy.wait_recv()
    unpack(0, to_conduct, C_ALL)
    set_coarse()
    for copy in first_out:
        copy.wait_recv()

    third = []
    for dg, src, dst in ((1, slice(4, 5), slice(2, 3)), (-1, slice(5, 6), slice(7, 8)),
                         (2, slice(4, 6), slice(0, 2)), (-2, slice(4, 6), slice(8, 10))):
        i = len(third)
        peer = (p, lax.rem(g + dg + n_grp, n_grp))
        third.append((0, dg, remote(u1.at[src, inner, :], u1.at[dst, inner, :], w_send.at[i], w_recv.at[i], peer)))
    start(second)
    start(third)
    unpack(1, to_basis, C_ALL)
    krylov(0, C_ALL)
    leave(first)
    for copy in conduct_out + first_out:
        copy.wait_send()
    arrive(second)
    set_diag((1, 8), MOST)
    set_weights((1, 2, 7, 8), (0, 1, 7, 8), MOST)
    arrive(third)
    leave(third)
    answer = coefficients(0)
    correct(u1, answer, range(5), C_ALL)
    sweep(u1, u0, range(1, 9), MOST)

    sweep(u0, u1, range(2, 8), MOST)
    sweep(u1, u0, range(3, 7), MOST)
    residual(u0, MOST)
    second_out = halve(2, 0.5, C_MOST)
    for copy in second_out:
        copy.start()
    for copy in second_out:
        copy.wait_recv()
    unpack(2, to_basis, C_MOST)
    krylov(1, C_MOST)
    leave(second)
    for copy in second_out:
        copy.wait_send()
    everyone(0).wait_send()
    answer = coefficients(1)
    correct(u0, answer, range(1, 4), C_MOST)
    sweep(u0, u1, range(4, 6), MINE)
    for w in range(2):
        out_ref[w, 0:PATCH, :] = u1[4 + w, FIRST:FIRST + PATCH, :]
        out_ref[w, PATCH:, :] = jnp.where(two, u1[4 + w, FIRST + PATCH:FIRST + OWN, :], 0.0)
    everyone(1).wait_send()


def solution(mesh):
    n_patch, n_grp = mesh.shape["patch"], mesh.shape["grp"]
    half = n_grp // 2

    def per_device(right_side, coefficient, row_counts):
        fine = pltpu.VMEM((WIDE, ROWS, LANES), F32)
        level = pltpu.VMEM((half, C_ROWS, LANES), F32)
        dma = pltpu.SemaphoreType.DMA
        return pl.pallas_call(
            functools.partial(kernel, n_patch, n_grp),
            out_shape=jax.ShapeDtypeStruct(right_side.shape, F32),
            in_specs=[
                pl.BlockSpec(memory_space=pltpu.HBM),
                pl.BlockSpec(memory_space=pltpu.HBM),
                pl.BlockSpec(memory_space=pltpu.HBM),
            ],
            out_specs=pl.BlockSpec(memory_space=pltpu.VMEM),
            scratch_shapes=[
                pltpu.VMEM(right_side.shape, right_side.dtype),
                pltpu.VMEM(coefficient.shape, coefficient.dtype),
                pltpu.SMEM(row_counts.shape, jnp.int32),
                dma((3,)),
                pltpu.VMEM((2, 2, OWN, LANES), F32),
                pltpu.VMEM((2, 2, HALO, LANES), F32),
                pltpu.VMEM((2, WIDE, HALO, LANES), F32),
                pltpu.VMEM((2, WIDE, HALO, LANES), F32),
                pltpu.VMEM((2, WIDE, ROWS, LANES), F32),
                fine, fine, fine, fine, fine, fine, fine,
                pltpu.VMEM((ROWS, LANES), F32),
                pltpu.VMEM((C_EXT, LANES), F32),
                pltpu.VMEM((3, C_SENT, LANES), F32),
                pltpu.VMEM((3, n_grp, C_SENT, LANES), F32),
                level, level, level, level, level,
                pltpu.VMEM((KRYLOV, half, C_ROWS, LANES), F32),
                pltpu.VMEM((CYCLES, 1, LANES), F32),
                pltpu.VMEM((CYCLES, n_patch, 1, LANES), F32),
                dma((22,)), dma((22,)), dma((4,)), dma((4,)), dma((4,)), dma((4,)),
                dma((3, n_grp)), dma((3, n_grp)),
                dma((CYCLES,)), dma((CYCLES,)),
            ],
            compiler_params=pltpu.CompilerParams(
                collective_id=0, has_side_effects=True, vmem_limit_bytes=40 << 20
            ),
        )(right_side, coefficient, row_counts)

    return jax.shard_map(
        per_device,
        mesh=mesh,
        in_specs=(P("grp", "patch", None), P("grp", "patch", None), P("patch")),
        out_specs=P("grp", "patch", None),
        check_vma=False,
    )
```

```python
import functools

import jax
import jax.numpy as jnp
from jax import lax
from jax.experimental import pallas as pl
from jax.experimental.pallas import tpu as pltpu
from jax.sharding import PartitionSpec as P

MESH = pl.DeviceIdType.MESH
CYCLES = 2
KRYLOV = 4
PATCH = 64
CAP = 2
OWN = 128
HALO = 24
EXT = OWN + 2 * HALO
GUARD = 8
ROWS = EXT + 2 * GUARD
FIRST = GUARD + HALO
WIDE = 10
LANES = 128
ALL = range(EXT // 8)
MOST = range(1, EXT // 8 - 1)
MINE = range(HALO // 8, (HALO + OWN) // 8)
C_EXT = EXT // 2
C_ROWS = C_EXT + 2 * GUARD
C_ALL = range(C_EXT // 8)
C_MOST = range(1, C_EXT // 8 - 1)
C_SENT = 48
F32 = jnp.float32
SIDE = 8


def lane_roll(x, steps):
    return pltpu.roll(x, steps % LANES, axis=1)


def loop(count, body):
    def step(i, carry):
        body(i)
        return carry

    lax.fori_loop(0, count, step, 0)


def each(tiles, body):
    for i in tiles:
        body(i)


def farthest_first(i):
    return SIDE // 2 + jnp.where(i % 2 == 0, i // 2, -((i + 1) // 2))


def at_tile(i, offset):
    return pl.ds(offset + 8 * i, 8)


def kernel(n_patch, n_grp, own, count_ref, out_ref,
            last, low, high, kf, gain, diag, cx, cy, cz, u0, u1, total, coarse, packed, gathered,
           kc, ccx, ccy, ccz, cdiag, basis, images, part, parts,
           p_send, p_recv, b_send, b_recv, w_send, w_recv, c_send, c_recv, s_send, s_recv):
    half = n_grp // 2
    p = lax.axis_index("patch")
    g = lax.axis_index("grp")
    lane = lax.broadcasted_iota(jnp.int32, (8, LANES), 1)
    row = lax.broadcasted_iota(jnp.int32, (8, LANES), 0)
    even = lane % 2 == 0
    zero = jnp.zeros((8, LANES), F32)

    def inside(dp, dg):
        return (p + dp >= 0) & (p + dp < n_patch) & (g + dg >= 0) & (g + dg < n_grp)

    barrier = pltpu.get_barrier_semaphore()
    for dp in (-1, 1):
        for dg in (0, -2, -1, 1, 2):
            peer = (lax.rem(p + dp + n_patch, n_patch), lax.rem(g + dg + n_grp, n_grp))
            pl.semaphore_signal(barrier, inc=1, device_id=peer, device_id_type=MESH)
    for dg in range(1, n_grp):
        pl.semaphore_signal(barrier, inc=1, device_id=(p, lax.rem(g + dg, n_grp)), device_id_type=MESH)

    def greet(i):
        peer = (lax.rem(p + i + 2, n_patch), g)
        pl.semaphore_signal(barrier, inc=1, device_id=peer, device_id_type=MESH)

    loop(n_patch - 3, greet)
    count = count_ref[0]
    two = count >= 2

    for a in range(2):
        for w in range(2):
            last[a, w] = jnp.where(two, own[a, w, OWN - HALO:, :], own[a, w, PATCH - HALO:PATCH, :])

    pl.semaphore_wait(barrier, n_patch + n_grp + 6)

    def remote(src, dst, send, recv, peer):
        return pltpu.make_async_remote_copy(
            src_ref=src, dst_ref=dst, send_sem=send, recv_sem=recv, device_id=peer, device_id_type=MESH
        )

    first = []
    for a in range(2):
        for dp, source, landing in ((0, own, kf), (1, last, low), (-1, own, high)):
            for dg in (-2, 2, -1, 1, 0):
                if (dp == 0 and dg == 0) or (a == 1 and abs(dg) == 2):
                    continue
                at = 4 - 2 * dg
                w = {2: slice(1, 2), -2: slice(0, 1)}.get(dg, slice(0, 2))
                src, dst = source.at[a, w], landing.at[a, at + w.start:at + w.stop]
                if dp == 0:
                    dst = landing.at[a, at + w.start:at + w.stop, FIRST:FIRST + OWN, :]
                elif dp == -1:
                    src = source.at[a, w, 0:HALO, :]
                peer = (lax.rem(p + dp + n_patch, n_patch), lax.rem(g + dg + n_grp, n_grp))
                i = len(first)
                first.append((dp, dg, remote(src, dst, p_send.at[i], p_recv.at[i], peer)))
    conduct_halo, source_halo = first[:14], first[14:]

    def start(copies):
        for dp, dg, copy in copies:
            @pl.when(inside(dp, dg))
            def _(copy=copy):
                copy.start()

    def arrive(copies):
        for dp, dg, copy in copies:
            @pl.when(inside(-dp, -dg))
            def _(copy=copy):
                copy.wait_recv()

    def leave(copies):
        for dp, dg, copy in copies:
            @pl.when(inside(dp, dg))
            def _(copy=copy):
                copy.wait_send()

    start(conduct_halo)
    start(source_halo)

    for a in range(2):
        for w in range(2):
            kf[a, 4 + w, FIRST:FIRST + OWN, :] = own[a, w]

    guards = jnp.zeros((GUARD, LANES), F32)
    for ref in (u0, u1, cy):
        for w in range(WIDE):
            ref[w, 0:GUARD, :] = guards
            ref[w, ROWS - GUARD:, :] = guards
    for w in range(WIDE):
        kf[0, w, 0:GUARD, :] = guards
        kf[0, w, ROWS - GUARD:, :] = guards
    for j in range(half):
        for ref in (kc, ccy):
            ref[j, 0:GUARD, :] = guards
            ref[j, C_ROWS - GUARD:, :] = guards
        for m in range(KRYLOV):
            basis[m, j, 0:GUARD, :] = guards
            basis[m, j, C_ROWS - GUARD:, :] = guards

    def clear(ref):
        ref[...] = jnp.zeros(ref.shape, ref.dtype)

    @pl.when(p == 0)
    def _():
        clear(low)

    @pl.when(p == n_patch - 1)
    def _():
        clear(high)

    def outside(planes):
        for w in planes:
            def wipe(i, w=w):
                rows = at_tile(i, 0)
                kf[0, w, rows, :] = zero
                kf[1, w, rows, :] = zero
                u1[w, rows, :] = zero

            loop(ROWS // 8, wipe)
            for a in range(2):
                for ref in (low, high):
                    ref[a, w] = jnp.zeros((HALO, LANES), F32)

    @pl.when(g < 2)
    def _():
        outside((0, 1))

    @pl.when(g < 1)
    def _():
        outside((2, 3))

    @pl.when(g > n_grp - 3)
    def _():
        outside((8, 9))

    @pl.when(g > n_grp - 2)
    def _():
        outside((6, 7))

    arrive(conduct_halo)

    def extend(a, w):
        kf[a, w, GUARD:FIRST, :] = low[a, w]
        upper = high[a, w]
        middle = slice(FIRST + PATCH, FIRST + PATCH + HALO)
        kf[a, w, middle, :] = jnp.where(two, kf[a, w, middle, :], upper)
        kf[a, w, FIRST + OWN:FIRST + OWN + HALO, :] = jnp.where(two, upper, 0.0)

    for w in range(1, 9):
        extend(0, w)

    inner = slice(GUARD + 8, GUARD + EXT - 8)
    second = []
    for dg, src, dst in ((2, (0, 4), (0, 0)), (-2, (0, 5), (0, 9)), (2, (1, 5), (1, 1)), (-2, (1, 4), (1, 8))):
        i = len(second)
        peer = (p, lax.rem(g + dg + n_grp, n_grp))
        second.append((0, dg, remote(
            kf.at[src[0], src[1], inner, :], kf.at[dst[0], dst[1], inner, :], b_send.at[i], b_recv.at[i], peer)))

    def halve(slot, scale, tiles):
        top, sent, skip = window(tiles)

        def fold(i):
            s = total[pl.ds(GUARD + 16 * i, 8, stride=2), :] + total[pl.ds(GUARD + 16 * i + 1, 8, stride=2), :]
            coarse[at_tile(i, 0), :] = scale * (s + jnp.where(even, lane_roll(s, -1), lane_roll(s, 1)))

        each(tiles, fold)

        def pack(i):
            value = jnp.where(even, coarse[at_tile(i, top), :], coarse[at_tile(i, top + skip), :])
            packed[slot, at_tile(i, 0), :] = value
            gathered[slot, g, at_tile(i, 0), :] = value

        each(range(sent // 8), pack)
        return [
            remote(packed.at[slot, 0:sent, :], gathered.at[slot, g, 0:sent, :], c_send.at[slot, dg],
                   c_recv.at[slot, dg], (p, lax.rem(g + dg, n_grp)))
            for dg in sorted(range(1, n_grp), key=lambda d: (-min(d, n_grp - d), d))
        ]

    def window(tiles):
        rows = 8 * len(tiles)
        sent = (rows // 2 + 7) // 8 * 8
        return 8 * tiles[0], sent, rows - sent

    def unpack(slot, write, tiles):
        top, sent, skip = window(tiles)

        def upper(i):
            for j in range(half):
                a, b = gathered[slot, j, at_tile(i, 0), :], gathered[slot, j + half, at_tile(i, 0), :]
                write(j, at_tile(i, GUARD + top), jnp.where(even, a, lane_roll(b, 1)))

        def lower(i):
            for j in range(half):
                rows = at_tile(i, sent - skip)
                a, b = gathered[slot, j, rows, :], gathered[slot, j + half, rows, :]
                write(j, at_tile(i, GUARD + top + sent), jnp.where(even, lane_roll(a, -1), b))

        each(range(sent // 8), upper)
        each(range(skip // 8), lower)

    def sum_conduct(i):
        rows = at_tile(i, GUARD)
        total[rows, :] = kf[0, 4, rows, :] + kf[0, 5, rows, :]

    each(ALL, sum_conduct)
    conduct_out = halve(0, 0.125, C_ALL)
    for copy in conduct_out:
        copy.start()

    def joined(a, b):
        return jnp.where((a > 0) & (b > 0), 0.5 * (a + b), 0.0)

    def set_diag(planes, tiles):
        def body(i):
            rows, before, after = at_tile(i, GUARD), at_tile(i, GUARD - 1), at_tile(i, GUARD + 1)
            for w in planes:
                k = kf[0, w, rows, :]
                near = kf[0, w - 1, rows, :] + kf[0, w + 1, rows, :] + kf[0, w, before, :] + kf[0, w, after, :]
                near = near + jnp.where(lane == LANES - 1, 0.0, lane_roll(k, -1))
                near = near + jnp.where(lane == 0, 0.0, lane_roll(k, 1))
                d = 3.0 * k + 0.5 * near
                diag[w, rows, :] = jnp.where(k > 0, d, 0.0)
                gain[w, rows, :] = jnp.where(k > 0, 0.8 / d, 0.0)

        each(tiles, body)

    def set_weights(planes, between, tiles):
        def body(i):
            rows, after = at_tile(i, GUARD), at_tile(i, GUARD + 1)
            for w in between:
                cx[w, rows, :] = joined(kf[0, w, rows, :], kf[0, w + 1, rows, :])
            for w in planes:
                k = kf[0, w, rows, :]
                cy[w, rows, :] = joined(k, kf[0, w, after, :])
                cz[w, rows, :] = jnp.where(lane == LANES - 1, 0.0, joined(k, lane_roll(k, -1)))

        each(tiles, body)

    def neighbours(u, i, planes):
        rows, before, after = at_tile(i, GUARD), at_tile(i, GUARD - 1), at_tile(i, GUARD + 1)
        centre = {w: u[w, rows, :] for w in range(planes[0] - 1, planes[-1] + 2)}
        result = {}
        for w in planes:
            z = cz[w, rows, :]
            s = cx[w, rows, :] * centre[w + 1] + cx[w - 1, rows, :] * centre[w - 1]
            s = s + cy[w, rows, :] * u[w, after, :] + cy[w, before, :] * u[w, before, :]
            s = s + z * lane_roll(centre[w], -1) + lane_roll(z * centre[w], 1)
            result[w] = s
        return rows, centre, result

    def sweep(src, dst, planes, tiles):
        def body(i):
            rows, centre, near = neighbours(src, i, planes)
            for w in planes:
                dst[w, rows, :] = 0.2 * centre[w] + gain[w, rows, :] * (kf[1, w, rows, :] + near[w])

        each(tiles, body)

    def residual(src, tiles):
        def body(i):
            rows, centre, near = neighbours(src, i, (4, 5))
            r = [kf[1, w, rows, :] - diag[w, rows, :] * centre[w] + near[w] for w in (4, 5)]
            total[rows, :] = r[0] + r[1]

        each(tiles, body)

    def set_coarse():
        def body(i):
            rows, before, after = at_tile(i, GUARD), at_tile(i, GUARD - 1), at_tile(i, GUARD + 1)
            k = [kc[j, rows, :] for j in range(half)]
            for j in range(half):
                beyond = k[j + 1] if j + 1 < half else jnp.where(even, lane_roll(k[0], -1), 0.0)
                ahead = k[j - 1] if j else jnp.where(even, 0.0, lane_roll(k[half - 1], 1))
                right = jnp.where(lane >= LANES - 2, 0.0, lane_roll(k[j], -2))
                left = jnp.where(lane < 2, 0.0, lane_roll(k[j], 2))
                up = kc[j, after, :]
                near = beyond + ahead + right + left + up + kc[j, before, :]
                cdiag[j, rows, :] = jnp.where(k[j] > 0, 3.0 * k[j] + 0.5 * near, 0.0)
                ccx[j, rows, :] = joined(k[j], beyond)
                ccy[j, rows, :] = joined(k[j], up)
                ccz[j, rows, :] = joined(k[j], right)

        each(C_ALL, body)

    def krylov(cycle, tiles):
        sums = []
        for m in range(KRYLOV):
            def body(i, carry, m=m):
                rows, before, after = at_tile(i, GUARD), at_tile(i, GUARD - 1), at_tile(i, GUARD + 1)
                at = row + 8 * i
                mine = (at >= HALO // 2) & (at < HALO // 2 + PATCH // 2 * count)
                v = [basis[m, j, rows, :] for j in range(half)]
                square, cross = carry
                for j in range(half):
                    x, z = ccx[j, rows, :], ccz[j, rows, :]
                    s = x * v[j + 1] if j + 1 < half else x * lane_roll(v[0], -1)
                    if j:
                        s = s + ccx[j - 1, rows, :] * v[j - 1]
                    else:
                        s = s + lane_roll(ccx[half - 1, rows, :] * v[half - 1], 1)
                    s = s + ccy[j, rows, :] * basis[m, j, after, :] + ccy[j, before, :] * basis[m, j, before, :]
                    s = s + z * lane_roll(v[j], -2) + lane_roll(z * v[j], 2)
                    mapped = cdiag[j, rows, :] * v[j] - s
                    if m + 1 < KRYLOV:
                        basis[m + 1, j, rows, :] = mapped
                    masked = jnp.where(mine, v[j], 0.0)
                    square = square + masked * v[j]
                    cross = cross + masked * mapped
                return square, cross

            carry = (zero, zero)
            for i in tiles:
                carry = body(i, carry)
            sums.extend(carry)
        stacked = jnp.concatenate([jnp.sum(value, axis=0, keepdims=True) for value in sums], axis=0)
        stacked = jnp.where(lane == row, jnp.sum(stacked, axis=1, keepdims=True), 0.0)
        line = jnp.sum(stacked, axis=0, keepdims=True)
        part[cycle] = line
        parts[cycle, p] = line

        def send(i):
            dz, dy = farthest_first(i // SIDE), farthest_first(i % SIDE)
            peer = (lax.rem(p // SIDE + dz, n_patch // SIDE) * SIDE + lax.rem(p % SIDE + dy, SIDE), g)
            remote(part.at[cycle], parts.at[cycle, p], s_send.at[cycle], s_recv.at[cycle], peer).start()

        loop(n_patch - 1, send)

    def everyone(cycle):
        rows = parts.at[cycle, 0:n_patch - 1]
        return remote(rows, rows, s_send.at[cycle], s_recv.at[cycle], (lax.rem(p + 1, n_patch), g))

    def coefficients(cycle):
        everyone(cycle).wait_recv()
        whole = jnp.sum(parts[cycle], axis=0)
        moment = [jnp.broadcast_to(whole[:, m:m + 1], (8, LANES)) for m in range(2 * KRYLOV)]
        matrix = [[moment[i + j + 1] for j in range(KRYLOV)] for i in range(KRYLOV)]
        right = moment[:KRYLOV]
        inverse = []
        for i in range(KRYLOV):
            pivot = matrix[i][i]
            inverse.append(jnp.where(pivot > 0, 1.0 / pivot, 0.0))
            for j in range(i + 1, KRYLOV):
                factor = matrix[i][j] * inverse[i]
                for l in range(j, KRYLOV):
                    matrix[j][l] = matrix[j][l] - factor * matrix[i][l]
                right[j] = right[j] - factor * right[i]
        answer = [None] * KRYLOV
        for i in reversed(range(KRYLOV)):
            value = right[i]
            for j in range(i + 1, KRYLOV):
                value = value - matrix[i][j] * answer[j]
            answer[i] = value * inverse[i]
        return answer

    def spread(u, weigh, slabs, tiles, add):
        for s in slabs:
            at = g + s - 2
            valid = (at >= 0) & (at < n_grp)
            at = lax.rem(at + n_grp, n_grp)
            j, odd = lax.rem(at, half), at // half

            def body(i, s=s, valid=valid, j=j, odd=odd):
                value = weigh(j, at_tile(i, GUARD))
                moved = jnp.where(odd == 0, lane_roll(value, 1), lane_roll(value, -1))
                value = jnp.where(lane % 2 == odd, value, moved)
                value = jnp.where(valid, value, 0.0)
                for w in (2 * s, 2 * s + 1):
                    for a in range(2):
                        rows = pl.ds(GUARD + 16 * i + a, 8, stride=2)
                        u[w, rows, :] = u[w, rows, :] + value if add else value

            each(tiles, body)

    def combined(answer):
        def weigh(j, rows):
            value = zero
            for m in range(KRYLOV):
                value = value + answer[m] * basis[m, j, rows, :]
            return value

        return weigh

    def to_basis(j, rows, value):
        basis[0, j, rows, :] = value

    def to_conduct(j, rows, value):
        kc[j, rows, :] = value

    set_diag(range(2, 8), ALL)
    set_weights(range(3, 7), range(2, 7), ALL)
    arrive(source_halo)
    for w in range(2, 8):
        extend(1, w)

    def sweep_zero(i):
        rows = at_tile(i, GUARD)
        for w in range(2, 8):
            u0[w, rows, :] = gain[w, rows, :] * kf[1, w, rows, :]

    each(ALL, sweep_zero)
    sweep(u0, u1, range(3, 7), ALL)
    residual(u1, ALL)
    first_out = halve(1, 0.5, C_ALL)
    for copy in first_out:
        copy.start()
    for copy in conduct_out:
        copy.wait_recv()
    unpack(0, to_conduct, C_ALL)
    set_coarse()
    for copy in first_out:
        copy.wait_recv()

    third = []
    for dg, src, dst in ((1, slice(4, 5), slice(2, 3)), (-1, slice(5, 6), slice(7, 8)),
                         (2, slice(4, 6), slice(0, 2)), (-2, slice(4, 6), slice(8, 10))):
        i = len(third)
        peer = (p, lax.rem(g + dg + n_grp, n_grp))
        third.append((0, dg, remote(u1.at[src, inner, :], u1.at[dst, inner, :], w_send.at[i], w_recv.at[i], peer)))
    start(second)
    start(third)
    unpack(1, to_basis, C_ALL)
    krylov(0, C_ALL)
    leave(first)
    for copy in conduct_out + first_out:
        copy.wait_send()
    arrive(second)
    set_diag((1, 8), MOST)
    set_weights((1, 2, 7, 8), (0, 1, 7, 8), MOST)
    arrive(third)
    leave(third)
    answer = coefficients(0)
    spread(u1, combined(answer), range(5), C_ALL, True)
    sweep(u1, u0, range(1, 9), MOST)

    sweep(u0, u1, range(2, 8), MOST)
    sweep(u1, u0, range(3, 7), MOST)
    residual(u0, MOST)
    second_out = halve(2, 0.5, C_MOST)
    for copy in second_out:
        copy.start()
    for copy in second_out:
        copy.wait_recv()
    unpack(2, to_basis, C_MOST)
    krylov(1, C_MOST)
    leave(second)
    for copy in second_out:
        copy.wait_send()
    everyone(0).wait_send()

    sweep(u0, u1, range(4, 6), MINE)
    for m in range(KRYLOV):
        spread(u0, lambda j, rows, m=m: basis[m, j, rows, :], range(1, 4), C_MOST, False)

        def image(i, m=m):
            rows, centre, near = neighbours(u0, i, (4, 5))
            for w in (4, 5):
                images[m, w - 4, rows, :] = 0.2 * centre[w] + gain[w, rows, :] * near[w]

        each(MINE, image)
    answer = coefficients(1)

    def finish(i):
        for w in range(2):
            value = u1[4 + w, at_tile(i, FIRST), :]
            for m in range(KRYLOV):
                value = value + answer[m] * images[m, w, at_tile(i, FIRST), :]
            if i >= PATCH // 8:
                value = jnp.where(two, value, 0.0)
            out_ref[w, at_tile(i, 0), :] = value

    each(range(OWN // 8), finish)
    everyone(1).wait_send()


def solution(mesh):
    n_patch, n_grp = mesh.shape["patch"], mesh.shape["grp"]
    half = n_grp // 2

    def per_device(right_side, coefficient, row_counts):
        fine = pltpu.VMEM((WIDE, ROWS, LANES), F32)
        level = pltpu.VMEM((half, C_ROWS, LANES), F32)
        dma = pltpu.SemaphoreType.DMA
        used = lax.broadcasted_iota(jnp.int32, (2,) + right_side.shape, 2) < PATCH * row_counts[0]
        own = jnp.where(used, jnp.stack([coefficient.astype(F32), right_side.astype(F32)]), 0.0)
        return pl.pallas_call(
            functools.partial(kernel, n_patch, n_grp),
            out_shape=jax.ShapeDtypeStruct(right_side.shape, F32),
            in_specs=[
                pl.BlockSpec(memory_space=pltpu.VMEM),
                pl.BlockSpec(memory_space=pltpu.SMEM),
            ],
            out_specs=pl.BlockSpec(memory_space=pltpu.VMEM),
            scratch_shapes=[
                pltpu.VMEM((2, 2, HALO, LANES), F32),
                pltpu.VMEM((2, WIDE, HALO, LANES), F32),
                pltpu.VMEM((2, WIDE, HALO, LANES), F32),
                pltpu.VMEM((2, WIDE, ROWS, LANES), F32),
                fine, fine, fine, fine, fine, fine, fine,
                pltpu.VMEM((ROWS, LANES), F32),
                pltpu.VMEM((C_EXT, LANES), F32),
                pltpu.VMEM((3, C_SENT, LANES), F32),
                pltpu.VMEM((3, n_grp, C_SENT, LANES), F32),
                level, level, level, level, level,
                pltpu.VMEM((KRYLOV, half, C_ROWS, LANES), F32),
                pltpu.VMEM((KRYLOV, 2, ROWS, LANES), F32),
                pltpu.VMEM((CYCLES, 1, LANES), F32),
                pltpu.VMEM((CYCLES, n_patch, 1, LANES), F32),
                dma((22,)), dma((22,)), dma((4,)), dma((4,)), dma((4,)), dma((4,)),
                dma((3, n_grp)), dma((3, n_grp)),
                dma((CYCLES,)), dma((CYCLES,)),
            ],
            compiler_params=pltpu.CompilerParams(
                collective_id=0, has_side_effects=True, vmem_limit_bytes=40 << 20
            ),
        )(own, row_counts)

    return jax.shard_map(
        per_device,
        mesh=mesh,
        in_specs=(P("grp", "patch", None), P("grp", "patch", None), P("patch")),
        out_specs=P("grp", "patch", None),
        check_vma=False,
    )
```

```python
import functools

import jax
import jax.numpy as jnp
from jax import lax
from jax.experimental import pallas as pl
from jax.experimental.pallas import tpu as pltpu
from jax.sharding import PartitionSpec as P

MESH = pl.DeviceIdType.MESH
CYCLES = 2
KRYLOV = 4
PATCH = 64
CAP = 2
OWN = 128
HALO = 24
EXT = OWN + 2 * HALO
GUARD = 8
ROWS = EXT + 2 * GUARD
FIRST = GUARD + HALO
WIDE = 10
LANES = 128
ALL = range(EXT // 8)
MOST = range(1, EXT // 8 - 1)
MINE = range(HALO // 8, (HALO + OWN) // 8)
C_EXT = EXT // 2
C_ROWS = C_EXT + 2 * GUARD
C_ALL = range(C_EXT // 8)
C_MOST = range(1, C_EXT // 8 - 1)
C_SENT = 48
F32 = jnp.float32
SIDE = 8


def lane_roll(x, steps):
    return pltpu.roll(x, steps % LANES, axis=1)


def loop(count, body):
    def step(i, carry):
        body(i)
        return carry

    lax.fori_loop(0, count, step, 0)


def each(tiles, body):
    for i in tiles:
        body(i)


def farthest_first(i):
    return SIDE // 2 + jnp.where(i % 2 == 0, i // 2, -((i + 1) // 2))


def at_tile(i, offset):
    return pl.ds(offset + 8 * i, 8)


def kernel(n_patch, n_grp, own, count_ref, out_ref,
            last, low, high, kf, gain, diag, cx, cy, cz, u0, u1, total, coarse, packed, gathered,
           kc, ccx, ccy, ccz, cdiag, basis, images, part, parts,
           p_send, p_recv, b_send, b_recv, w_send, w_recv, c_send, c_recv, s_send, s_recv):
    half = n_grp // 2
    p = lax.axis_index("patch")
    g = lax.axis_index("grp")
    lane = lax.broadcasted_iota(jnp.int32, (8, LANES), 1)
    row = lax.broadcasted_iota(jnp.int32, (8, LANES), 0)
    even = lane % 2 == 0
    zero = jnp.zeros((8, LANES), F32)

    def inside(dp, dg):
        return (p + dp >= 0) & (p + dp < n_patch) & (g + dg >= 0) & (g + dg < n_grp)

    barrier = pltpu.get_barrier_semaphore()
    for dp in (-1, 1):
        for dg in (0, -2, -1, 1, 2):
            peer = (lax.rem(p + dp + n_patch, n_patch), lax.rem(g + dg + n_grp, n_grp))
            pl.semaphore_signal(barrier, inc=1, device_id=peer, device_id_type=MESH)
    for dg in range(1, n_grp):
        pl.semaphore_signal(barrier, inc=1, device_id=(p, lax.rem(g + dg, n_grp)), device_id_type=MESH)

    def greet(i):
        peer = (lax.rem(p + i + 2, n_patch), g)
        pl.semaphore_signal(barrier, inc=1, device_id=peer, device_id_type=MESH)

    loop(n_patch - 3, greet)
    count = count_ref[0]
    two = count >= 2

    for a in range(2):
        for w in range(2):
            last[a, w] = jnp.where(two, own[a, w, OWN - HALO:, :], own[a, w, PATCH - HALO:PATCH, :])

    pl.semaphore_wait(barrier, n_patch + n_grp + 6)

    def remote(src, dst, send, recv, peer):
        return pltpu.make_async_remote_copy(
            src_ref=src, dst_ref=dst, send_sem=send, recv_sem=recv, device_id=peer, device_id_type=MESH
        )

    first = []
    for a in range(2):
        for dp, source, landing in ((0, own, kf), (1, last, low), (-1, own, high)):
            for dg in (-2, 2, -1, 1, 0):
                if (dp == 0 and dg == 0) or (a == 1 and abs(dg) == 2):
                    continue
                at = 4 - 2 * dg
                w = {2: slice(1, 2), -2: slice(0, 1)}.get(dg, slice(0, 2))
                src, dst = source.at[a, w], landing.at[a, at + w.start:at + w.stop]
                if dp == 0:
                    dst = landing.at[a, at + w.start:at + w.stop, FIRST:FIRST + OWN, :]
                elif dp == -1:
                    src = source.at[a, w, 0:HALO, :]
                peer = (lax.rem(p + dp + n_patch, n_patch), lax.rem(g + dg + n_grp, n_grp))
                i = len(first)
                first.append((dp, dg, remote(src, dst, p_send.at[i], p_recv.at[i], peer)))
    conduct_halo, source_halo = first[:14], first[14:]
    near_halo = [c for c in conduct_halo if abs(c[1]) < 2]
    far_halo = [c for c in conduct_halo if abs(c[1]) == 2]

    def start(copies):
        for dp, dg, copy in copies:
            @pl.when(inside(dp, dg))
            def _(copy=copy):
                copy.start()

    def arrive(copies):
        for dp, dg, copy in copies:
            @pl.when(inside(-dp, -dg))
            def _(copy=copy):
                copy.wait_recv()

    def leave(copies):
        for dp, dg, copy in copies:
            @pl.when(inside(dp, dg))
            def _(copy=copy):
                copy.wait_send()

    start(near_halo)
    start(far_halo)
    start(source_halo)

    for a in range(2):
        for w in range(2):
            kf[a, 4 + w, FIRST:FIRST + OWN, :] = own[a, w]

    guards = jnp.zeros((GUARD, LANES), F32)
    for ref in (u0, u1, cy):
        for w in range(WIDE):
            ref[w, 0:GUARD, :] = guards
            ref[w, ROWS - GUARD:, :] = guards
    for w in range(WIDE):
        kf[0, w, 0:GUARD, :] = guards
        kf[0, w, ROWS - GUARD:, :] = guards
    for j in range(half):
        for ref in (kc, ccy):
            ref[j, 0:GUARD, :] = guards
            ref[j, C_ROWS - GUARD:, :] = guards
        for m in range(KRYLOV):
            basis[m, j, 0:GUARD, :] = guards
            basis[m, j, C_ROWS - GUARD:, :] = guards

    def clear(ref):
        ref[...] = jnp.zeros(ref.shape, ref.dtype)

    @pl.when(p == 0)
    def _():
        clear(low)

    @pl.when(p == n_patch - 1)
    def _():
        clear(high)

    def outside(planes):
        for w in planes:
            def wipe(i, w=w):
                rows = at_tile(i, 0)
                kf[0, w, rows, :] = zero
                kf[1, w, rows, :] = zero
                u1[w, rows, :] = zero

            loop(ROWS // 8, wipe)
            for a in range(2):
                for ref in (low, high):
                    ref[a, w] = jnp.zeros((HALO, LANES), F32)

    @pl.when(g < 2)
    def _():
        outside((0, 1))

    @pl.when(g < 1)
    def _():
        outside((2, 3))

    @pl.when(g > n_grp - 3)
    def _():
        outside((8, 9))

    @pl.when(g > n_grp - 2)
    def _():
        outside((6, 7))

    arrive(near_halo)

    def extend(a, w):
        kf[a, w, GUARD:FIRST, :] = low[a, w]
        upper = high[a, w]
        middle = slice(FIRST + PATCH, FIRST + PATCH + HALO)
        kf[a, w, middle, :] = jnp.where(two, kf[a, w, middle, :], upper)
        kf[a, w, FIRST + OWN:FIRST + OWN + HALO, :] = jnp.where(two, upper, 0.0)

    for w in range(2, 8):
        extend(0, w)

    inner = slice(GUARD + 8, GUARD + EXT - 8)
    second = []
    for dg, src, dst in ((2, (0, 4), (0, 0)), (-2, (0, 5), (0, 9)), (2, (1, 5), (1, 1)), (-2, (1, 4), (1, 8))):
        i = len(second)
        peer = (p, lax.rem(g + dg + n_grp, n_grp))
        second.append((0, dg, remote(
            kf.at[src[0], src[1], inner, :], kf.at[dst[0], dst[1], inner, :], b_send.at[i], b_recv.at[i], peer)))

    def halve(slot, scale, tiles):
        top, sent, skip = window(tiles)

        def fold(i):
            s = total[pl.ds(GUARD + 16 * i, 8, stride=2), :] + total[pl.ds(GUARD + 16 * i + 1, 8, stride=2), :]
            coarse[at_tile(i, 0), :] = scale * (s + jnp.where(even, lane_roll(s, -1), lane_roll(s, 1)))

        each(tiles, fold)

        def pack(i):
            value = jnp.where(even, coarse[at_tile(i, top), :], coarse[at_tile(i, top + skip), :])
            packed[slot, at_tile(i, 0), :] = value
            gathered[slot, g, at_tile(i, 0), :] = value

        each(range(sent // 8), pack)
        return [
            remote(packed.at[slot, 0:sent, :], gathered.at[slot, g, 0:sent, :], c_send.at[slot, dg],
                   c_recv.at[slot, dg], (p, lax.rem(g + dg, n_grp)))
            for dg in sorted(range(1, n_grp), key=lambda d: (-min(d, n_grp - d), d))
        ]

    def window(tiles):
        rows = 8 * len(tiles)
        sent = (rows // 2 + 7) // 8 * 8
        return 8 * tiles[0], sent, rows - sent

    def unpack(slot, write, tiles):
        top, sent, skip = window(tiles)

        def upper(i):
            for j in range(half):
                a, b = gathered[slot, j, at_tile(i, 0), :], gathered[slot, j + half, at_tile(i, 0), :]
                write(j, at_tile(i, GUARD + top), jnp.where(even, a, lane_roll(b, 1)))

        def lower(i):
            for j in range(half):
                rows = at_tile(i, sent - skip)
                a, b = gathered[slot, j, rows, :], gathered[slot, j + half, rows, :]
                write(j, at_tile(i, GUARD + top + sent), jnp.where(even, lane_roll(a, -1), b))

        each(range(sent // 8), upper)
        each(range(skip // 8), lower)

    def sum_conduct(i):
        rows = at_tile(i, GUARD)
        total[rows, :] = kf[0, 4, rows, :] + kf[0, 5, rows, :]

    each(ALL, sum_conduct)
    conduct_out = halve(0, 0.125, C_ALL)
    for copy in conduct_out:
        copy.start()

    def joined(a, b):
        return jnp.where((a > 0) & (b > 0), 0.5 * (a + b), 0.0)

    def set_diag(planes, tiles):
        def body(i):
            rows, before, after = at_tile(i, GUARD), at_tile(i, GUARD - 1), at_tile(i, GUARD + 1)
            for w in planes:
                k = kf[0, w, rows, :]
                near = kf[0, w - 1, rows, :] + kf[0, w + 1, rows, :] + kf[0, w, before, :] + kf[0, w, after, :]
                near = near + jnp.where(lane == LANES - 1, 0.0, lane_roll(k, -1))
                near = near + jnp.where(lane == 0, 0.0, lane_roll(k, 1))
                d = 3.0 * k + 0.5 * near
                diag[w, rows, :] = jnp.where(k > 0, d, 0.0)
                gain[w, rows, :] = jnp.where(k > 0, 0.8 / d, 0.0)

        each(tiles, body)

    def set_weights(planes, between, tiles):
        def body(i):
            rows, after = at_tile(i, GUARD), at_tile(i, GUARD + 1)
            for w in between:
                cx[w, rows, :] = joined(kf[0, w, rows, :], kf[0, w + 1, rows, :])
            for w in planes:
                k = kf[0, w, rows, :]
                cy[w, rows, :] = joined(k, kf[0, w, after, :])
                cz[w, rows, :] = jnp.where(lane == LANES - 1, 0.0, joined(k, lane_roll(k, -1)))

        each(tiles, body)

    def neighbours(u, i, planes):
        rows, before, after = at_tile(i, GUARD), at_tile(i, GUARD - 1), at_tile(i, GUARD + 1)
        centre = {w: u[w, rows, :] for w in range(planes[0] - 1, planes[-1] + 2)}
        result = {}
        for w in planes:
            z = cz[w, rows, :]
            s = cx[w, rows, :] * centre[w + 1] + cx[w - 1, rows, :] * centre[w - 1]
            s = s + cy[w, rows, :] * u[w, after, :] + cy[w, before, :] * u[w, before, :]
            s = s + z * lane_roll(centre[w], -1) + lane_roll(z * centre[w], 1)
            result[w] = s
        return rows, centre, result

    def sweep(src, dst, planes, tiles):
        def body(i):
            rows, centre, near = neighbours(src, i, planes)
            for w in planes:
                dst[w, rows, :] = 0.2 * centre[w] + gain[w, rows, :] * (kf[1, w, rows, :] + near[w])

        each(tiles, body)

    def residual(src, tiles):
        def body(i):
            rows, centre, near = neighbours(src, i, (4, 5))
            r = [kf[1, w, rows, :] - diag[w, rows, :] * centre[w] + near[w] for w in (4, 5)]
            total[rows, :] = r[0] + r[1]

        each(tiles, body)

    def set_coarse():
        def body(i):
            rows, before, after = at_tile(i, GUARD), at_tile(i, GUARD - 1), at_tile(i, GUARD + 1)
            k = [kc[j, rows, :] for j in range(half)]
            for j in range(half):
                beyond = k[j + 1] if j + 1 < half else jnp.where(even, lane_roll(k[0], -1), 0.0)
                ahead = k[j - 1] if j else jnp.where(even, 0.0, lane_roll(k[half - 1], 1))
                right = jnp.where(lane >= LANES - 2, 0.0, lane_roll(k[j], -2))
                left = jnp.where(lane < 2, 0.0, lane_roll(k[j], 2))
                up = kc[j, after, :]
                near = beyond + ahead + right + left + up + kc[j, before, :]
                cdiag[j, rows, :] = jnp.where(k[j] > 0, 3.0 * k[j] + 0.5 * near, 0.0)
                ccx[j, rows, :] = joined(k[j], beyond)
                ccy[j, rows, :] = joined(k[j], up)
                ccz[j, rows, :] = joined(k[j], right)

        each(C_ALL, body)

    def krylov(cycle, tiles):
        sums = []
        for m in range(KRYLOV):
            def body(i, carry, m=m):
                rows, before, after = at_tile(i, GUARD), at_tile(i, GUARD - 1), at_tile(i, GUARD + 1)
                at = row + 8 * i
                mine = (at >= HALO // 2) & (at < HALO // 2 + PATCH // 2 * count)
                v = [basis[m, j, rows, :] for j in range(half)]
                square, cross = carry
                for j in range(half):
                    x, z = ccx[j, rows, :], ccz[j, rows, :]
                    s = x * v[j + 1] if j + 1 < half else x * lane_roll(v[0], -1)
                    if j:
                        s = s + ccx[j - 1, rows, :] * v[j - 1]
                    else:
                        s = s + lane_roll(ccx[half - 1, rows, :] * v[half - 1], 1)
                    s = s + ccy[j, rows, :] * basis[m, j, after, :] + ccy[j, before, :] * basis[m, j, before, :]
                    s = s + z * lane_roll(v[j], -2) + lane_roll(z * v[j], 2)
                    mapped = cdiag[j, rows, :] * v[j] - s
                    if m + 1 < KRYLOV:
                        basis[m + 1, j, rows, :] = mapped
                    masked = jnp.where(mine, v[j], 0.0)
                    square = square + masked * v[j]
                    cross = cross + masked * mapped
                return square, cross

            carry = (zero, zero)
            for i in tiles:
                carry = body(i, carry)
            sums.extend(carry)
        stacked = jnp.concatenate([jnp.sum(value, axis=0, keepdims=True) for value in sums], axis=0)
        stacked = jnp.where(lane == row, jnp.sum(stacked, axis=1, keepdims=True), 0.0)
        line = jnp.sum(stacked, axis=0, keepdims=True)
        part[cycle] = line
        parts[cycle, p] = line

        def send(i):
            dz, dy = farthest_first(i // SIDE), farthest_first(i % SIDE)
            peer = (lax.rem(p // SIDE + dz, n_patch // SIDE) * SIDE + lax.rem(p % SIDE + dy, SIDE), g)
            remote(part.at[cycle], parts.at[cycle, p], s_send.at[cycle], s_recv.at[cycle], peer).start()

        loop(n_patch - 1, send)

    def everyone(cycle):
        rows = parts.at[cycle, 0:n_patch - 1]
        return remote(rows, rows, s_send.at[cycle], s_recv.at[cycle], (lax.rem(p + 1, n_patch), g))

    def coefficients(cycle):
        everyone(cycle).wait_recv()
        whole = jnp.sum(parts[cycle], axis=0)
        moment = [jnp.broadcast_to(whole[:, m:m + 1], (8, LANES)) for m in range(2 * KRYLOV)]
        matrix = [[moment[i + j + 1] for j in range(KRYLOV)] for i in range(KRYLOV)]
        right = moment[:KRYLOV]
        inverse = []
        for i in range(KRYLOV):
            pivot = matrix[i][i]
            inverse.append(jnp.where(pivot > 0, 1.0 / pivot, 0.0))
            for j in range(i + 1, KRYLOV):
                factor = matrix[i][j] * inverse[i]
                for l in range(j, KRYLOV):
                    matrix[j][l] = matrix[j][l] - factor * matrix[i][l]
                right[j] = right[j] - factor * right[i]
        answer = [None] * KRYLOV
        for i in reversed(range(KRYLOV)):
            value = right[i]
            for j in range(i + 1, KRYLOV):
                value = value - matrix[i][j] * answer[j]
            answer[i] = value * inverse[i]
        return answer

    def spread(u, weigh, slabs, tiles, add):
        for s in slabs:
            at = g + s - 2
            valid = (at >= 0) & (at < n_grp)
            at = lax.rem(at + n_grp, n_grp)
            j, odd = lax.rem(at, half), at // half

            def body(i, s=s, valid=valid, j=j, odd=odd):
                value = weigh(j, at_tile(i, GUARD))
                moved = jnp.where(odd == 0, lane_roll(value, 1), lane_roll(value, -1))
                value = jnp.where(lane % 2 == odd, value, moved)
                value = jnp.where(valid, value, 0.0)
                for w in (2 * s, 2 * s + 1):
                    for a in range(2):
                        rows = pl.ds(GUARD + 16 * i + a, 8, stride=2)
                        u[w, rows, :] = u[w, rows, :] + value if add else value

            each(tiles, body)

    def combined(answer):
        def weigh(j, rows):
            value = zero
            for m in range(KRYLOV):
                value = value + answer[m] * basis[m, j, rows, :]
            return value

        return weigh

    def to_basis(j, rows, value):
        basis[0, j, rows, :] = value

    def to_conduct(j, rows, value):
        kc[j, rows, :] = value

    set_weights(range(3, 7), range(2, 7), ALL)
    arrive(far_halo)
    for w in (1, 8):
        extend(0, w)
    set_diag(range(2, 8), ALL)
    arrive(source_halo)
    for w in range(2, 8):
        extend(1, w)

    def sweep_zero(i):
        rows = at_tile(i, GUARD)
        for w in range(2, 8):
            u0[w, rows, :] = gain[w, rows, :] * kf[1, w, rows, :]

    each(ALL, sweep_zero)
    sweep(u0, u1, range(3, 7), ALL)
    residual(u1, ALL)
    first_out = halve(1, 0.5, C_ALL)
    for copy in first_out:
        copy.start()
    for copy in conduct_out:
        copy.wait_recv()
    unpack(0, to_conduct, C_ALL)
    set_coarse()
    for copy in first_out:
        copy.wait_recv()

    third = []
    for dg, src, dst in ((1, slice(4, 5), slice(2, 3)), (-1, slice(5, 6), slice(7, 8)),
                         (2, slice(4, 6), slice(0, 2)), (-2, slice(4, 6), slice(8, 10))):
        i = len(third)
        peer = (p, lax.rem(g + dg + n_grp, n_grp))
        third.append((0, dg, remote(u1.at[src, inner, :], u1.at[dst, inner, :], w_send.at[i], w_recv.at[i], peer)))
    start(second)
    start(third)
    unpack(1, to_basis, C_ALL)
    krylov(0, C_ALL)
    leave(first)
    for copy in conduct_out + first_out:
        copy.wait_send()
    arrive(second)
    set_diag((1, 8), MOST)
    set_weights((1, 2, 7, 8), (0, 1, 7, 8), MOST)
    arrive(third)
    leave(third)
    answer = coefficients(0)
    spread(u1, combined(answer), range(5), C_ALL, True)
    sweep(u1, u0, range(1, 9), MOST)

    sweep(u0, u1, range(2, 8), MOST)
    sweep(u1, u0, range(3, 7), MOST)
    residual(u0, MOST)
    second_out = halve(2, 0.5, C_MOST)
    for copy in second_out:
        copy.start()
    for copy in second_out:
        copy.wait_recv()
    unpack(2, to_basis, C_MOST)
    krylov(1, C_MOST)
    leave(second)
    for copy in second_out:
        copy.wait_send()
    everyone(0).wait_send()

    sweep(u0, u1, range(4, 6), MINE)
    for m in range(KRYLOV):
        spread(u0, lambda j, rows, m=m: basis[m, j, rows, :], range(1, 4), C_MOST, False)

        def image(i, m=m):
            rows, centre, near = neighbours(u0, i, (4, 5))
            for w in (4, 5):
                images[m, w - 4, rows, :] = 0.2 * centre[w] + gain[w, rows, :] * near[w]

        each(MINE, image)
    answer = coefficients(1)

    def finish(i):
        for w in range(2):
            value = u1[4 + w, at_tile(i, FIRST), :]
            for m in range(KRYLOV):
                value = value + answer[m] * images[m, w, at_tile(i, FIRST), :]
            if i >= PATCH // 8:
                value = jnp.where(two, value, 0.0)
            out_ref[w, at_tile(i, 0), :] = value

    each(range(OWN // 8), finish)
    everyone(1).wait_send()


def solution(mesh):
    n_patch, n_grp = mesh.shape["patch"], mesh.shape["grp"]
    half = n_grp // 2

    def per_device(right_side, coefficient, row_counts):
        fine = pltpu.VMEM((WIDE, ROWS, LANES), F32)
        level = pltpu.VMEM((half, C_ROWS, LANES), F32)
        dma = pltpu.SemaphoreType.DMA
        used = lax.broadcasted_iota(jnp.int32, (2,) + right_side.shape, 2) < PATCH * row_counts[0]
        own = jnp.where(used, jnp.stack([coefficient.astype(F32), right_side.astype(F32)]), 0.0)
        return pl.pallas_call(
            functools.partial(kernel, n_patch, n_grp),
            out_shape=jax.ShapeDtypeStruct(right_side.shape, F32),
            in_specs=[
                pl.BlockSpec(memory_space=pltpu.VMEM),
                pl.BlockSpec(memory_space=pltpu.SMEM),
            ],
            out_specs=pl.BlockSpec(memory_space=pltpu.VMEM),
            scratch_shapes=[
                pltpu.VMEM((2, 2, HALO, LANES), F32),
                pltpu.VMEM((2, WIDE, HALO, LANES), F32),
                pltpu.VMEM((2, WIDE, HALO, LANES), F32),
                pltpu.VMEM((2, WIDE, ROWS, LANES), F32),
                fine, fine, fine, fine, fine, fine, fine,
                pltpu.VMEM((ROWS, LANES), F32),
                pltpu.VMEM((C_EXT, LANES), F32),
                pltpu.VMEM((3, C_SENT, LANES), F32),
                pltpu.VMEM((3, n_grp, C_SENT, LANES), F32),
                level, level, level, level, level,
                pltpu.VMEM((KRYLOV, half, C_ROWS, LANES), F32),
                pltpu.VMEM((KRYLOV, 2, ROWS, LANES), F32),
                pltpu.VMEM((CYCLES, 1, LANES), F32),
                pltpu.VMEM((CYCLES, n_patch, 1, LANES), F32),
                dma((22,)), dma((22,)), dma((4,)), dma((4,)), dma((4,)), dma((4,)),
                dma((3, n_grp)), dma((3, n_grp)),
                dma((CYCLES,)), dma((CYCLES,)),
            ],
            compiler_params=pltpu.CompilerParams(
                collective_id=0, has_side_effects=True, vmem_limit_bytes=40 << 20
            ),
        )(own, row_counts)

    return jax.shard_map(
        per_device,
        mesh=mesh,
        in_specs=(P("grp", "patch", None), P("grp", "patch", None), P("patch")),
        out_specs=P("grp", "patch", None),
        check_vma=False,
    )
```
